256 devices in a mesh: ctx: 64 (over x, z, core), section: 4 (over y).
Axes of the slice: x: 4, y: 4, z: 8, core: 2. Of those that a mesh axis runs over, the one named last changes fastest.
Arguments:
- query_heads: bfloat16 [4, 8192, 4096], P('section', 'ctx'), may hold values from -12 to 12
- key_heads: bfloat16 [4, 8192, 512], P('section', 'ctx'), may hold values from -12 to 12
- value_heads: bfloat16 [4, 8192, 512], P('section', 'ctx'), may hold values from -6 to 6
- attn_output: bfloat16 [4, 8192, 4096], P('section', 'ctx'), may hold values from -6 to 6
- output_grad: bfloat16 [4, 8192, 4096], P('section', 'ctx'), may hold values from -6 to 6
- doc_start: int32 [8192], P('ctx'), may hold values from 0 to 8191, as said below
- fetch_list: int32 [64, 2], P('ctx'), may hold values from 0 to 1, as said below
Outputs:
- handed_grad: bfloat16 [4, 8192, 4096], P('section', 'ctx')
- key_grad: bfloat16 [4, 8192, 512], P('section', 'ctx')
- value_grad: bfloat16 [4, 8192, 512], P('section', 'ctx')
The draws below stay inside these ranges and needn't reach their ends.
Inputs may be any that keep to these rules, and one draw needn't show every extreme that they name: doc_start never falls, doc_start[t] <= t, and positions with equal doc_start form one document; a document holds at most 257 positions, and some hold exactly that many; the last position forms a document of its own. fetch_list[i, d - 1] is 1 exactly when some position of shard i and some position of shard i - d lie in one document.
All inputs are finite; a program needn't handle non-finite values.
Results may differ from the reference program's by a relative error of at most 0.0095.
Values may be sent and summed in bfloat16 or wider, within the bound.
A program may use at most 64 MiB of HBM per device.

```python
import math
import jax
import jax.numpy as jnp
from jax import lax

HQ = 32
HK = 4
HD = 128
TOK_DEV = 128
FETCH = 2
SEQ = 8192
LAYERS = 4
N_CTX = 64


def document_layout(key):
    total_len = SEQ
    longest = FETCH * TOK_DEV + 1
    pick_key, long_key, short_key = jax.random.split(jax.random.fold_in(key, 101), 3)
    is_long = jax.random.randint(pick_key, (total_len,), 0, 2)
    long_len = jax.random.randint(long_key, (total_len,), TOK_DEV, longest + 1)
    short_len = jax.random.randint(short_key, (total_len,), 1, max(TOK_DEV // 2, 2) + 1)
    order_idx = jnp.arange(total_len, dtype=jnp.int32)
    lengths = jnp.where(is_long == 1, long_len, short_len)
    lengths = jnp.where(order_idx % 4 == 0, longest, lengths)
    starts = jnp.cumsum(lengths) - lengths
    inside = starts < total_len
    marks = jnp.zeros((total_len,), jnp.int32).at[jnp.where(inside, starts, 0)].max(inside.astype(jnp.int32))
    marks = jnp.where(order_idx == total_len - 1, 1, marks)
    doc_begin = lax.cummax(marks * order_idx, axis=0)
    first_begin = doc_begin[::TOK_DEV]
    shard_ids = jnp.arange(N_CTX, dtype=jnp.int32)
    distance = jnp.arange(1, FETCH + 1, dtype=jnp.int32)
    source = shard_ids[:, None] - distance[None, :]
    fetched = ((source >= 0) & (first_begin[:, None] < (source + 1) * TOK_DEV)).astype(jnp.int32)
    return (doc_begin.astype(jnp.int32), fetched)


def draw_doc_start(key, part):
    return document_layout(key)[0]


def draw_fetch_list(key, part):
    return document_layout(key)[1]


def draw_key_heads(key, part):
    key = jax.random.fold_in(key, 2)
    base = jnp.clip(jax.random.normal(key, (LAYERS, SEQ, HK * HD), jnp.float32), -4.0, 4.0)
    return base.astype(jnp.bfloat16)


def draw_query_heads(key, part):
    key = jax.random.fold_in(key, 1)
    base = jnp.clip(jax.random.normal(key, (LAYERS, SEQ, HQ * HD), jnp.float32), -4.0, 4.0)
    return base.astype(jnp.bfloat16)


def shard_levels(rng, dims, shards, low, high):
    def one(position, parts):
        steps = jax.random.uniform(jax.random.fold_in(jax.random.fold_in(rng, 6), position), (parts,), jnp.float32, low / len(shards), high / len(shards))
        return jnp.repeat(jnp.exp(steps), dims[position] // parts).reshape((-1,) + (1,) * (len(dims) - position - 1))

    factor_of = one(*shards[0])
    for cut in shards[1:]:
        factor_of = factor_of * one(*cut)
    return factor_of


def scatter_about(rng, extent, deviation, bound, cuts=(), kind=jnp.bfloat16):
    loudness = shard_levels(rng, extent, cuts, -0.22, 0.18) if cuts else 1.0
    values = jax.random.normal(rng, extent, jnp.float32) * deviation * loudness
    return jnp.minimum(jnp.maximum(values, -bound), bound).astype(kind)


def setup_inputs(seed: int = 0) -> dict:
    streams_of = jax.random.split(jax.random.key(seed), 8)
    query_heads = draw_query_heads(jax.random.fold_in(streams_of[7], 71), 0)
    key_heads = draw_key_heads(jax.random.fold_in(streams_of[7], 71), 0)
    value_heads = scatter_about(streams_of[2], (LAYERS, SEQ, HK * HD), 1.0, 6.0, ((0, 4), (1, 64)))
    attn_output = scatter_about(streams_of[3], (LAYERS, SEQ, HQ * HD), 1.0, 6.0, ((0, 4), (1, 64)))
    output_grad = scatter_about(streams_of[4], (LAYERS, SEQ, HQ * HD), 1.0, 6.0, ((0, 4), (1, 64)))
    doc_start = draw_doc_start(jax.random.fold_in(streams_of[7], 71), 0)
    fetch_list = draw_fetch_list(jax.random.fold_in(streams_of[7], 71), 0)
    return {"query_heads": query_heads, "key_heads": key_heads, "value_heads": value_heads, "attn_output": attn_output, "output_grad": output_grad, "doc_start": doc_start, "fetch_list": fetch_list}


ROPE_BASE = 1000000.0
TRAINED_CONTEXT = 32768.0
YARN_FACTOR = 4.0
NEG_LARGE = -1.0e30


def yarn_frequencies(head_dim):
    half_dim = head_dim // 2

    def correction(rotations):
        return head_dim * math.log(TRAINED_CONTEXT / (rotations * 2.0 * math.pi)) / (2.0 * math.log(ROPE_BASE))

    lower_dim = max(math.floor(correction(32.0)), 0)
    upper_dim = min(math.ceil(correction(1.0)), head_dim - 1)
    spread_dims = max(upper_dim - lower_dim, 0.001)
    indices = jnp.arange(half_dim, dtype=jnp.float32)
    extrapolated = jnp.power(jnp.float32(ROPE_BASE), -2.0 * indices / head_dim)
    ramp_weight = jnp.clip((indices - lower_dim) / spread_dims, 0.0, 1.0)
    return extrapolated / YARN_FACTOR * ramp_weight + extrapolated * (1.0 - ramp_weight)


def rope_tables(positions, head_dim):
    freqs = yarn_frequencies(head_dim)
    angles = positions.astype(jnp.float32)[:, None] * freqs[None, :]
    angles = jnp.concatenate([angles, angles], axis=1)
    factor = 0.1 * math.log(YARN_FACTOR) + 1.0
    return (jnp.cos(angles) * factor)[:, None, :], (jnp.sin(angles) * factor)[:, None, :]


def apply_rope(inputs, cosine, sine_table):
    half_dim = inputs.shape[-1] // 2
    turned = jnp.concatenate([-inputs[..., half_dim:], inputs[..., :half_dim]], axis=-1)
    return inputs * cosine + turned * sine_table


def undo_rope(grads, cosine, sine_table):
    half_dim = grads.shape[-1] // 2
    scaled = grads * sine_table
    return grads * cosine + jnp.concatenate([scaled[..., half_dim:], -scaled[..., :half_dim]], axis=-1)


def layer_grads(query_heads, key_heads, value_heads, attn_output, output_grad, doc_start, fetch_list):
    seq_len = query_heads.shape[0]
    ratio = HQ // HK
    score_scale = HD ** -0.5
    span = (FETCH + 1) * TOK_DEV
    front = FETCH * TOK_DEV
    positions = jnp.arange(seq_len, dtype=jnp.int32) - doc_start
    cosine, sine_table = rope_tables(positions, HD)
    q_rot = apply_rope(query_heads.astype(jnp.float32).reshape(seq_len, HQ, HD), cosine, sine_table)
    q_rot = q_rot.astype(jnp.bfloat16).reshape(seq_len, HK, ratio, HD)
    k_rot = apply_rope(key_heads.astype(jnp.float32).reshape(seq_len, HK, HD), cosine, sine_table).astype(jnp.bfloat16)
    val_rows = value_heads.reshape(seq_len, HK, HD)
    grad_rows = output_grad.reshape(seq_len, HK, ratio, HD)
    delta = jnp.sum((output_grad.astype(jnp.float32) * attn_output.astype(jnp.float32)).reshape(seq_len, HK, ratio, HD), axis=-1)
    k_pad = jnp.concatenate([jnp.zeros((front, HK, HD), jnp.bfloat16), k_rot], axis=0)
    v_pad = jnp.concatenate([jnp.zeros((front, HK, HD), jnp.bfloat16), val_rows], axis=0)
    window_idx = jnp.arange(span, dtype=jnp.int32)
    block_idx = jnp.arange(TOK_DEV, dtype=jnp.int32)

    def shard_step(carry, shard_index):
        dk_acc, dv_acc = carry
        row_start = shard_index * TOK_DEV
        q_blk = lax.dynamic_slice_in_dim(q_rot, row_start, TOK_DEV, 0).astype(jnp.float32)
        g_blk = lax.dynamic_slice_in_dim(grad_rows, row_start, TOK_DEV, 0).astype(jnp.float32)
        d_blk = lax.dynamic_slice_in_dim(delta, row_start, TOK_DEV, 0)
        s_blk = lax.dynamic_slice_in_dim(doc_start, row_start, TOK_DEV, 0)
        k_win = lax.dynamic_slice_in_dim(k_pad, row_start, span, 0).astype(jnp.float32)
        v_win = lax.dynamic_slice_in_dim(v_pad, row_start, span, 0).astype(jnp.float32)
        t_pos = row_start + block_idx
        u_pos = row_start - front + window_idx
        offset = FETCH - window_idx // TOK_DEV
        table = jnp.concatenate([jnp.ones((1,), jnp.int32), fetch_list[shard_index]], axis=0)
        listed = table[offset]
        allowed = (u_pos[None, :] >= s_blk[:, None]) & (u_pos[None, :] <= t_pos[:, None]) & (listed[None, :] == 1)
        pair_mask = allowed[:, None, None, :]
        scores = jnp.einsum("tgre,uge->tgru", q_blk, k_win) * score_scale
        largest = jnp.max(jnp.where(pair_mask, scores, NEG_LARGE), axis=-1)
        exp_total = jnp.sum(jnp.where(pair_mask, jnp.exp(scores - largest[..., None]), 0.0), axis=-1)
        lse = largest + jnp.log(exp_total)
        prob = jnp.where(pair_mask, jnp.exp(scores - lse[..., None]), 0.0)
        prob_b = prob.astype(jnp.bfloat16)
        dprob = jnp.einsum("tgre,uge->tgru", g_blk, v_win)
        dscore = (prob * (dprob - d_blk[..., None])).astype(jnp.bfloat16).astype(jnp.float32)
        dq_blk = jnp.einsum("tgru,uge->tgre", dscore, k_win) * score_scale
        dk_win = jnp.einsum("tgru,tgre->uge", dscore, q_blk) * score_scale
        dv_win = jnp.einsum("tgru,tgre->uge", prob_b.astype(jnp.float32), g_blk)
        dk_acc = lax.dynamic_update_slice_in_dim(dk_acc, lax.dynamic_slice_in_dim(dk_acc, row_start, span, 0) + dk_win, row_start, 0)
        dv_acc = lax.dynamic_update_slice_in_dim(dv_acc, lax.dynamic_slice_in_dim(dv_acc, row_start, span, 0) + dv_win, row_start, 0)
        return (dk_acc, dv_acc), dq_blk

    start_acc = jnp.zeros((seq_len + front, HK, HD), jnp.float32)
    (dk_acc, dv_acc), dq_blocks = lax.scan(shard_step, (start_acc, start_acc), jnp.arange(seq_len // TOK_DEV, dtype=jnp.int32))
    dq_rot = dq_blocks.reshape(seq_len, HQ, HD)
    query_grad = undo_rope(dq_rot, cosine, sine_table).astype(jnp.bfloat16).reshape(seq_len, HQ * HD)
    key_grad = undo_rope(dk_acc[front:], cosine, sine_table).astype(jnp.bfloat16).reshape(seq_len, HK * HD)
    value_grad = dv_acc[front:].astype(jnp.bfloat16).reshape(seq_len, HK * HD)
    return query_grad, key_grad, value_grad


def reference(query_heads, key_heads, value_heads, attn_output, output_grad, doc_start, fetch_list):
    def per_layer(stacked):
        return layer_grads(stacked[0], stacked[1], stacked[2], stacked[3], stacked[4], doc_start, fetch_list)

    query_grad, key_grad, value_grad = lax.map(per_layer, (query_heads, key_heads, value_heads, attn_output, output_grad))
    handed_grad = jnp.concatenate([query_grad[1:], jnp.zeros_like(query_grad[:1])], axis=0)
    return handed_grad, key_grad, value_grad
```

```python
import functools
import math

import jax
import jax.numpy as jnp
import numpy as np
from jax import lax
from jax.experimental import pallas as pl
from jax.experimental.pallas import tpu as pltpu
from jax.sharding import PartitionSpec as P

HQ = 32
HK = 4
HD = 128
TOK = 128
RATIO = HQ // HK
PAIRS = RATIO // 2
HALF = HD // 2
ROPE_BASE = 1000000.0
TRAINED_CONTEXT = 32768.0
YARN_FACTOR = 4.0
NEG_LARGE = -1.0e30
SCALE = HD**-0.5
LONG = 0
MESH = pl.DeviceIdType.MESH
F32 = jnp.float32
BF16 = jnp.bfloat16


def yarn_frequencies():
    def correction(rotations):
        return HD * math.log(TRAINED_CONTEXT / (rotations * 2.0 * math.pi)) / (2.0 * math.log(ROPE_BASE))

    lower = max(math.floor(correction(32.0)), 0)
    upper = min(math.ceil(correction(1.0)), HD - 1)
    spread = max(upper - lower, 0.001)
    index = np.arange(HALF, dtype=np.float64)
    base = ROPE_BASE ** (-2.0 * index / HD)
    ramp = np.clip((index - lower) / spread, 0.0, 1.0)
    return (base / YARN_FACTOR * ramp + base * (1.0 - ramp)).astype(np.float32)


def sin_cos(x):
    n = jnp.floor(x * (2.0 / math.pi) + 0.5)
    r = x - n * 1.5703125
    r = r - n * 4.83751296997070312e-4
    r = r - n * 7.54978995489188216e-8
    z = r * r
    sin = r + r * z * (-1.6666654611e-1 + z * (8.3321608736e-3 + z * -1.9515295891e-4))
    cos = 1.0 - 0.5 * z + z * z * (4.166664568298827e-2 + z * (-1.388731625493765e-3 + z * 2.443315711809948e-5))
    q = n.astype(jnp.int32) & 3
    odd = (q & 1) == 1
    s = jnp.where(odd, cos, sin)
    c = jnp.where(odd, sin, cos)
    return jnp.where(q >= 2, -s, s), jnp.where((q == 1) | (q == 2), -c, c)


def dot_t(a, b):
    return lax.dot_general(a, b, (((1,), (1,)), ((), ())), preferred_element_type=F32)


def dot(a, b):
    return jnp.dot(a, b, preferred_element_type=F32)


def kernel(
    n_ctx,
    doc_ref, fetch_ref, freq_ref, q_hbm, k_hbm, v_hbm, o_hbm, do_hbm,
    out_ref, dk_ref, dv_ref,
    q_in, k_in, o_in, do_in,
    kv, qr, doz, bias, tab_t, tab_c, tab_s, k_t, p_win, ds_win, own, back_out, back_in, dq, relay,
    in_sem, kv_send, kv_recv, back_send, back_recv, dq_send, out_recv, relay_recv, relay_send,
):
    c = lax.axis_index("ctx")
    s = lax.axis_index("section")

    loads = [pltpu.make_async_copy(k_hbm.at[0], k_in, in_sem.at[0])]
    for g in range(HK):
        loads.append(pltpu.make_async_copy(v_hbm.at[0, :, pl.ds(g * HD, HD)], kv.at[0, g, 1], in_sem.at[1 + g]))
    loads.append(pltpu.make_async_copy(q_hbm.at[0], q_in, in_sem.at[5]))
    loads.append(pltpu.make_async_copy(do_hbm.at[0], do_in, in_sem.at[6]))
    loads.append(pltpu.make_async_copy(o_hbm.at[0], o_in, in_sem.at[7]))
    for load in loads:
        load.start()

    barrier = pltpu.get_barrier_semaphore()
    for d in (1, 2):
        @pl.when(c >= d)
        def _():
            pl.semaphore_signal(barrier, inc=1, device_id=(c - d, s), device_id_type=MESH)
    for me, others in ((0, (1, 2, 3)), (1, (0, 2)), (2, (0, 1, 3))):
        @pl.when(s == me)
        def _():
            for other in others:
                pl.semaphore_signal(barrier, inc=1, device_id=(c, other), device_id_type=MESH)

    first = c * TOK
    lane_t = lax.broadcasted_iota(jnp.int32, (1, TOK), 1) + first
    start = doc_ref[...]
    factor = 0.1 * math.log(YARN_FACTOR) + 1.0
    sin, cos = sin_cos((lane_t - start).astype(F32) * freq_ref[...])
    sin = sin * factor
    cos = cos * factor
    tab_t[0] = cos * SCALE
    tab_t[1] = sin * SCALE
    turned = jnp.concatenate([cos, sin], axis=0).T
    swapped = pltpu.roll(turned, HALF, 1)
    low = lax.broadcasted_iota(jnp.int32, (TOK, HD), 1) < HALF
    tab_c[...] = jnp.where(low, turned, swapped)
    tab_s[...] = jnp.where(low, -swapped, turned)

    def rope(x):
        x = x.astype(F32)
        return (x * tab_c[...] + pltpu.roll(x, HALF, 1) * tab_s[...]).astype(BF16)

    loads[0].wait()
    for g in range(HK):
        kv[0, g, 0] = rope(k_in[:, g * HD : (g + 1) * HD])
    for g in range(HK):
        loads[1 + g].wait()

    pl.semaphore_wait(
        barrier, 2 + (c < n_ctx - 1).astype(jnp.int32) + (c < n_ctx - 2).astype(jnp.int32)
    )

    def kv_copy(g, d):
        return pltpu.make_async_remote_copy(
            src_ref=kv.at[0, g], dst_ref=kv.at[d, g],
            send_sem=kv_send.at[d - 1, g], recv_sem=kv_recv.at[d - 1, g],
            device_id=(c + d, s), device_id_type=MESH,
        )

    for g in range(HK):
        for d in (1, 2):
            pl.when(c < n_ctx - d)(kv_copy(g, d).start)
    for d in (1, 2):
        @pl.when(c < d)
        def _():
            kv[d] = jnp.zeros((HK, 2, TOK, HD), BF16)
        @pl.when(c >= n_ctx - d)
        def _():
            back_in[d - 1] = jnp.zeros((HK, 2, TOK, HD), BF16)

    def zero_copy(p):
        return pltpu.make_async_copy(
            relay.at[0, 0], out_ref.at[0, :, pl.ds(pl.multiple_of(p * 2 * HD, 2 * HD), 2 * HD)], out_recv.at[p]
        )

    @pl.when(s == 3)
    def _():
        relay[0, 0] = jnp.zeros((TOK, 2 * HD), BF16)

        def put(p, carry):
            zero_copy(p).start()
            return carry

        lax.fori_loop(0, HK * PAIRS, put, 0)

    row = lax.broadcasted_iota(jnp.int32, (TOK, TOK), 0)
    for d in range(3):
        u = first - d * TOK + row
        allowed = (u >= start) & (u <= lane_t)
        if d > 0:
            allowed = allowed & (fetch_ref[:, d - 1 : d] == 1)
        bias[d * TOK : (d + 1) * TOK, :] = jnp.where(allowed, 0.0, NEG_LARGE)

    loads[5].wait()
    loads[6].wait()
    loads[7].wait()

    def prepare(h, carry):
        cols = pl.ds(pl.multiple_of(h * HD, HD), HD)
        qr[h] = rope(q_in[:, cols])
        grad = do_in[:, cols]
        prod = grad.astype(F32) * o_in[:, cols].astype(F32)
        prod = prod + pltpu.roll(prod, HALF, 1)
        high = prod.astype(BF16).astype(F32)
        doz[h, :, 0:HD] = grad
        doz[h, :, HD : 2 * HD] = jnp.where(low, high, prod - high).astype(BF16)
        return carry

    lax.fori_loop(0, HQ, prepare, 0)

    def out_cols(p):
        return out_ref.at[0, :, pl.ds(pl.multiple_of(p * 2 * HD, 2 * HD), 2 * HD)]

    def direct_copy(p):
        return pltpu.make_async_remote_copy(
            src_ref=dq.at[p], dst_ref=out_cols(p), send_sem=dq_send.at[p], recv_sem=out_recv.at[p],
            device_id=(c, s - 1), device_id_type=MESH,
        )

    def long_copy(g):
        return pltpu.make_async_remote_copy(
            src_ref=dq.at[g * PAIRS + LONG], dst_ref=relay.at[s // 3, g],
            send_sem=dq_send.at[g * PAIRS + LONG], recv_sem=relay_recv.at[s // 3, g],
            device_id=(c, 2 * (1 - s // 2)), device_id_type=MESH,
        )

    def relay_copy(slot, g, target):
        p = g * PAIRS + LONG
        return pltpu.make_async_remote_copy(
            src_ref=relay.at[slot, g], dst_ref=out_cols(p),
            send_sem=relay_send.at[slot, g], recv_sem=out_recv.at[p],
            device_id=(c, target), device_id_type=MESH,
        )

    def arrival(slot, g):
        return pltpu.make_async_remote_copy(
            src_ref=dq.at[g * PAIRS + LONG], dst_ref=relay.at[slot, g],
            send_sem=dq_send.at[g * PAIRS + LONG], recv_sem=relay_recv.at[slot, g],
            device_id=(c, 0), device_id_type=MESH,
        )

    def forward(g):
        @pl.when(s == 0)
        def _():
            arrival(0, g).wait_recv()
            relay_copy(0, g, 1).start()
            arrival(1, g).wait_recv()
            relay_copy(1, g, 2).start()

        @pl.when(s == 2)
        def _():
            arrival(0, g).wait_recv()
            relay_copy(0, g, 0).start()

    def back_copy(g, d):
        return pltpu.make_async_remote_copy(
            src_ref=back_out.at[d - 1, g], dst_ref=back_in.at[d - 1, g],
            send_sem=back_send.at[d - 1, g], recv_sem=back_recv.at[d - 1, g],
            device_id=(c - d, s), device_id_type=MESH,
        )

    def group(g, carry):
        for d in (1, 2):
            pl.when(c >= d)(kv_copy(g, d).wait_recv)
        k_win = jnp.concatenate([kv[d, g, 0] for d in range(3)], axis=0)
        v_win = jnp.concatenate([kv[d, g, 1] for d in range(3)], axis=0)
        v_one = jnp.concatenate([v_win, jnp.full((3 * TOK, HD), -1.0, BF16)], axis=1)
        k_t[...] = k_win.T
        for j in range(PAIRS):
            p = g * PAIRS + j
            h = g * RATIO + 2 * j
            qp = qr[pl.ds(h, 2)].reshape(2 * TOK, HD)
            dp_in = doz[pl.ds(h, 2)].reshape(2 * TOK, 2 * HD)
            sc = dot_t(k_win, qp) * (SCALE * math.log2(math.e))
            b = bias[...]
            sc = sc + jnp.concatenate([b, b], axis=1)
            e = jnp.exp2(sc - jnp.max(sc, axis=0, keepdims=True))
            prob = e * (1.0 / jnp.sum(e, axis=0, keepdims=True))
            ds = (prob * dot_t(v_one, dp_in)).astype(BF16)
            p_win[:, 2 * j * TOK : 2 * (j + 1) * TOK] = prob.astype(BF16)
            ds_win[:, 2 * j * TOK : 2 * (j + 1) * TOK] = ds
            turned_grad = dot(k_t[...], ds)
            for i in range(2):
                x = turned_grad[:HALF, i * TOK : (i + 1) * TOK]
                y = turned_grad[HALF:, i * TOK : (i + 1) * TOK]
                grad = jnp.concatenate(
                    [x * tab_t[0] + y * tab_t[1], y * tab_t[0] - x * tab_t[1]], axis=0
                )
                dq[p, :, i * HD : (i + 1) * HD] = grad.T.astype(BF16)

            @pl.when(s >= 1)
            def _():
                if j == LONG:
                    long_copy(g).start()
                else:
                    direct_copy(p).start()

        dk = dot(ds_win[...], qr[pl.ds(g * RATIO, RATIO)].reshape(RATIO * TOK, HD))
        dv = dot(p_win[...], doz[pl.ds(g * RATIO, RATIO), :, 0:HD].reshape(RATIO * TOK, HD))
        own[g, 0] = dk[:TOK]
        own[g, 1] = dv[:TOK]
        for d in (1, 2):
            back_out[d - 1, g, 0] = dk[d * TOK : (d + 1) * TOK].astype(BF16)
            back_out[d - 1, g, 1] = dv[d * TOK : (d + 1) * TOK].astype(BF16)
            pl.when(c >= d)(back_copy(g, d).start)

        @pl.when(g >= 1)
        def _():
            forward(g - 1)

        return carry

    lax.fori_loop(0, HK, group, 0)
    forward(HK - 1)

    def finish(g, carry):
        for d in (1, 2):
            pl.when(c < n_ctx - d)(back_copy(g, d).wait_recv)
        dk = own[g, 0] + back_in[0, g, 0].astype(F32) + back_in[1, g, 0].astype(F32)
        dv = own[g, 1] + back_in[0, g, 1].astype(F32) + back_in[1, g, 1].astype(F32)
        dk = dk * SCALE
        cols = pl.ds(pl.multiple_of(g * HD, HD), HD)
        dk_ref[0, :, cols] = (dk * tab_c[...] - pltpu.roll(dk, HALF, 1) * tab_s[...]).astype(BF16)
        dv_ref[0, :, cols] = dv.astype(BF16)
        return carry

    lax.fori_loop(0, HK, finish, 0)

    def drain(g, carry):
        for d in (1, 2):
            pl.when(c < n_ctx - d)(kv_copy(g, d).wait_send)
            pl.when(c >= d)(back_copy(g, d).wait_send)

        @pl.when(s >= 1)
        def _():
            for j in range(PAIRS):
                direct_copy(g * PAIRS + j).wait_send()

        @pl.when(s == 0)
        def _():
            relay_copy(0, g, 1).wait_send()
            relay_copy(1, g, 2).wait_send()

        @pl.when(s == 2)
        def _():
            relay_copy(0, g, 0).wait_send()

        @pl.when(s <= 2)
        def _():
            for j in range(PAIRS):
                direct_copy(g * PAIRS + j).wait_recv()

        @pl.when(s == 3)
        def _():
            for j in range(PAIRS):
                zero_copy(g * PAIRS + j).wait()

        return carry

    lax.fori_loop(0, HK, drain, 0)


def solution(mesh):
    n_ctx = mesh.shape["ctx"]
    freq = np.broadcast_to(yarn_frequencies()[:, None], (HALF, TOK)).copy()

    def shards(q, k, v, o, do, doc_start, fetch_list):
        any_spec = pl.BlockSpec(memory_space=pl.ANY)
        vmem = pl.BlockSpec(memory_space=pltpu.VMEM)
        dma = pltpu.SemaphoreType.DMA
        return pl.pallas_call(
            functools.partial(kernel, n_ctx),
            out_shape=(
                jax.ShapeDtypeStruct((1, TOK, HQ * HD), BF16),
                jax.ShapeDtypeStruct((1, TOK, HK * HD), BF16),
                jax.ShapeDtypeStruct((1, TOK, HK * HD), BF16),
            ),
            in_specs=[vmem] * 3 + [any_spec] * 5,
            out_specs=(any_spec, vmem, vmem),
            scratch_shapes=[
                pltpu.VMEM((TOK, HQ * HD), BF16),
                pltpu.VMEM((TOK, HK * HD), BF16),
                pltpu.VMEM((TOK, HQ * HD), BF16),
                pltpu.VMEM((TOK, HQ * HD), BF16),
                pltpu.VMEM((3, HK, 2, TOK, HD), BF16),
                pltpu.VMEM((HQ, TOK, HD), BF16),
                pltpu.VMEM((HQ, TOK, 2 * HD), BF16),
                pltpu.VMEM((3 * TOK, TOK), F32),
                pltpu.VMEM((2, HALF, TOK), F32),
                pltpu.VMEM((TOK, HD), F32),
                pltpu.VMEM((TOK, HD), F32),
                pltpu.VMEM((HD, 3 * TOK), BF16),
                pltpu.VMEM((3 * TOK, RATIO * TOK), BF16),
                pltpu.VMEM((3 * TOK, RATIO * TOK), BF16),
                pltpu.VMEM((HK, 2, TOK, HD), F32),
                pltpu.VMEM((2, HK, 2, TOK, HD), BF16),
                pltpu.VMEM((2, HK, 2, TOK, HD), BF16),
                pltpu.VMEM((HK * PAIRS, TOK, 2 * HD), BF16),
                pltpu.VMEM((2, HK, TOK, 2 * HD), BF16),
                dma((8,)),
                dma((2, HK)),
                dma((2, HK)),
                dma((2, HK)),
                dma((2, HK)),
                dma((HK * PAIRS,)),
                dma((HK * PAIRS,)),
                dma((2, HK)),
                dma((2, HK)),
            ],
            compiler_params=pltpu.CompilerParams(
                collective_id=0, has_side_effects=True, vmem_limit_bytes=24 << 20
            ),
            cost_estimate=pl.CostEstimate(flops=2_000_000_000, bytes_accessed=5_000_000, transcendentals=1_600_000),
        )(doc_start.reshape(1, TOK), fetch_list, jnp.asarray(freq), q, k, v, o, do)

    return jax.shard_map(
        shards,
        mesh=mesh,
        in_specs=(
            P("section", "ctx", None),
            P("section", "ctx", None),
            P("section", "ctx", None),
            P("section", "ctx", None),
            P("section", "ctx", None),
            P("ctx"),
            P("ctx", None),
        ),
        out_specs=(P("section", "ctx", None),) * 3,
        check_vma=False,
    )
```

```python
import functools
import math

import jax
import jax.numpy as jnp
import numpy as np
from jax import lax
from jax.experimental import pallas as pl
from jax.experimental.pallas import tpu as pltpu
from jax.sharding import PartitionSpec as P

HQ = 32
HK = 4
HD = 128
TOK = 128
RATIO = HQ // HK
PAIRS = RATIO // 2
HALF = HD // 2
ROPE_BASE = 1000000.0
TRAINED_CONTEXT = 32768.0
YARN_FACTOR = 4.0
NEG_LARGE = -1.0e30
SCALE = HD**-0.5
LONG = 0
N_LONG = 3
MESH = pl.DeviceIdType.MESH
F32 = jnp.float32
BF16 = jnp.bfloat16


def yarn_frequencies():
    def correction(rotations):
        return HD * math.log(TRAINED_CONTEXT / (rotations * 2.0 * math.pi)) / (2.0 * math.log(ROPE_BASE))

    lower = max(math.floor(correction(32.0)), 0)
    upper = min(math.ceil(correction(1.0)), HD - 1)
    spread = max(upper - lower, 0.001)
    index = np.arange(HALF, dtype=np.float64)
    base = ROPE_BASE ** (-2.0 * index / HD)
    ramp = np.clip((index - lower) / spread, 0.0, 1.0)
    return (base / YARN_FACTOR * ramp + base * (1.0 - ramp)).astype(np.float32)


def sin_cos(x):
    n = jnp.floor(x * (2.0 / math.pi) + 0.5)
    r = x - n * 1.5703125
    r = r - n * 4.83751296997070312e-4
    r = r - n * 7.54978995489188216e-8
    z = r * r
    sin = r + r * z * (-1.6666654611e-1 + z * (8.3321608736e-3 + z * -1.9515295891e-4))
    cos = 1.0 - 0.5 * z + z * z * (4.166664568298827e-2 + z * (-1.388731625493765e-3 + z * 2.443315711809948e-5))
    q = n.astype(jnp.int32) & 3
    odd = (q & 1) == 1
    s = jnp.where(odd, cos, sin)
    c = jnp.where(odd, sin, cos)
    return jnp.where(q >= 2, -s, s), jnp.where((q == 1) | (q == 2), -c, c)


def dot_t(a, b):
    return lax.dot_general(a, b, (((1,), (1,)), ((), ())), preferred_element_type=F32)


def dot(a, b):
    return jnp.dot(a, b, preferred_element_type=F32)


def kernel(
    n_ctx,
    doc_hbm, fetch_hbm, freq_hbm, q_hbm, k_hbm, v_hbm, o_hbm, do_hbm,
    out_ref, dk_ref, dv_ref,
    doc_ref, fetch_ref, freq_ref, q_in, k_in, o_in, do_in,
    kv, qr, doz, bias, tab_t, tab_c, tab_s, k_t, p_win, ds_win, own, back_out, back_in, dq, relay,
    in_sem, kv_send, kv_recv, back_send, back_recv, dq_send, out_recv, relay_recv, relay_send,
):
    c = lax.axis_index("ctx")
    s = lax.axis_index("section")

    loads = [pltpu.make_async_copy(k_hbm.at[0], k_in, in_sem.at[0])]
    for g in range(HK):
        loads.append(pltpu.make_async_copy(v_hbm.at[0, :, pl.ds(g * HD, HD)], kv.at[0, g, 1], in_sem.at[1 + g]))
    loads.append(pltpu.make_async_copy(q_hbm.at[0], q_in, in_sem.at[5]))
    loads.append(pltpu.make_async_copy(do_hbm.at[0], do_in, in_sem.at[6]))
    loads.append(pltpu.make_async_copy(o_hbm.at[0], o_in, in_sem.at[7]))
    small = [
        pltpu.make_async_copy(doc_hbm, doc_ref, in_sem.at[8]),
        pltpu.make_async_copy(freq_hbm, freq_ref, in_sem.at[9]),
        pltpu.make_async_copy(fetch_hbm, fetch_ref, in_sem.at[10]),
    ]
    for load in small + loads:
        load.start()

    barrier = pltpu.get_barrier_semaphore()
    for d in (1, 2):
        @pl.when(c >= d)
        def _():
            pl.semaphore_signal(barrier, inc=1, device_id=(c - d, s), device_id_type=MESH)
    for me, others in ((0, (1, 2, 3)), (1, (0, 2)), (2, (0, 1, 3))):
        @pl.when(s == me)
        def _():
            for other in others:
                pl.semaphore_signal(barrier, inc=1, device_id=(c, other), device_id_type=MESH)

    first = c * TOK
    lane_t = lax.broadcasted_iota(jnp.int32, (1, TOK), 1) + first
    for load in small:
        load.wait()
    start = doc_ref[...]
    factor = 0.1 * math.log(YARN_FACTOR) + 1.0
    sin, cos = sin_cos((lane_t - start).astype(F32) * freq_ref[...])
    sin = sin * factor
    cos = cos * factor
    tab_t[0] = cos * SCALE
    tab_t[1] = sin * SCALE
    turned = jnp.concatenate([cos, sin], axis=0).T
    swapped = pltpu.roll(turned, HALF, 1)
    low = lax.broadcasted_iota(jnp.int32, (TOK, HD), 1) < HALF
    tab_c[...] = jnp.where(low, turned, swapped)
    tab_s[...] = jnp.where(low, -swapped, turned)

    def rope(x):
        x = x.astype(F32)
        return (x * tab_c[...] + pltpu.roll(x, HALF, 1) * tab_s[...]).astype(BF16)

    loads[0].wait()
    for g in range(HK):
        kv[0, g, 0] = rope(k_in[:, g * HD : (g + 1) * HD])
    for g in range(HK):
        loads[1 + g].wait()

    pl.semaphore_wait(
        barrier, 2 + (c < n_ctx - 1).astype(jnp.int32) + (c < n_ctx - 2).astype(jnp.int32)
    )

    def kv_copy(g, d):
        return pltpu.make_async_remote_copy(
            src_ref=kv.at[0, g], dst_ref=kv.at[d, g],
            send_sem=kv_send.at[d - 1, g], recv_sem=kv_recv.at[d - 1, g],
            device_id=(c + d, s), device_id_type=MESH,
        )

    for g in range(HK):
        for d in (1, 2):
            pl.when(c < n_ctx - d)(kv_copy(g, d).start)
    for d in (1, 2):
        @pl.when(c < d)
        def _():
            kv[d] = jnp.zeros((HK, 2, TOK, HD), BF16)
        @pl.when(c >= n_ctx - d)
        def _():
            back_in[d - 1] = jnp.zeros((HK, 2, TOK, HD), BF16)

    def zero_copy(p):
        return pltpu.make_async_copy(
            relay.at[0, 0], out_ref.at[0, :, pl.ds(pl.multiple_of(p * 2 * HD, 2 * HD), 2 * HD)], out_recv.at[p]
        )

    @pl.when(s == 3)
    def _():
        relay[0, 0] = jnp.zeros((TOK, 2 * HD), BF16)

        def put(p, carry):
            zero_copy(p).start()
            return carry

        lax.fori_loop(0, HK * PAIRS, put, 0)

    row = lax.broadcasted_iota(jnp.int32, (TOK, TOK), 0)
    for d in range(3):
        u = first - d * TOK + row
        allowed = (u >= start) & (u <= lane_t)
        if d > 0:
            allowed = allowed & (fetch_ref[:, d - 1 : d] == 1)
        bias[d * TOK : (d + 1) * TOK, :] = jnp.where(allowed, 0.0, NEG_LARGE)

    loads[5].wait()
    loads[6].wait()
    loads[7].wait()

    def prepare(h, carry):
        cols = pl.ds(pl.multiple_of(h * HD, HD), HD)
        qr[h] = rope(q_in[:, cols])
        grad = do_in[:, cols]
        prod = grad.astype(F32) * o_in[:, cols].astype(F32)
        prod = prod + pltpu.roll(prod, HALF, 1)
        high = prod.astype(BF16).astype(F32)
        doz[h, :, 0:HD] = grad
        doz[h, :, HD : 2 * HD] = jnp.where(low, high, prod - high).astype(BF16)
        return carry

    lax.fori_loop(0, HQ, prepare, 0)

    def out_cols(p):
        return out_ref.at[0, :, pl.ds(pl.multiple_of(p * 2 * HD, 2 * HD), 2 * HD)]

    def direct_copy(p):
        return pltpu.make_async_remote_copy(
            src_ref=dq.at[p], dst_ref=out_cols(p), send_sem=dq_send.at[p], recv_sem=out_recv.at[p],
            device_id=(c, s - 1), device_id_type=MESH,
        )

    def long_copy(g):
        return pltpu.make_async_remote_copy(
            src_ref=dq.at[g * PAIRS + LONG], dst_ref=relay.at[s // 3, g],
            send_sem=dq_send.at[g * PAIRS + LONG], recv_sem=relay_recv.at[s // 3, g],
            device_id=(c, 2 * (1 - s // 2)), device_id_type=MESH,
        )

    def relay_copy(slot, g, target):
        p = g * PAIRS + LONG
        return pltpu.make_async_remote_copy(
            src_ref=relay.at[slot, g], dst_ref=out_cols(p),
            send_sem=relay_send.at[slot, g], recv_sem=out_recv.at[p],
            device_id=(c, target), device_id_type=MESH,
        )

    def arrival(slot, g):
        return pltpu.make_async_remote_copy(
            src_ref=dq.at[g * PAIRS + LONG], dst_ref=relay.at[slot, g],
            send_sem=dq_send.at[g * PAIRS + LONG], recv_sem=relay_recv.at[slot, g],
            device_id=(c, 0), device_id_type=MESH,
        )

    def forward(g):
        @pl.when(s == 0)
        def _():
            arrival(0, g).wait_recv()
            relay_copy(0, g, 1).start()
            arrival(1, g).wait_recv()
            relay_copy(1, g, 2).start()

        @pl.when(s == 2)
        def _():
            arrival(0, g).wait_recv()
            relay_copy(0, g, 0).start()

    def back_copy(g, d):
        return pltpu.make_async_remote_copy(
            src_ref=back_out.at[d - 1, g], dst_ref=back_in.at[d - 1, g],
            send_sem=back_send.at[d - 1, g], recv_sem=back_recv.at[d - 1, g],
            device_id=(c - d, s), device_id_type=MESH,
        )

    def group(g, carry):
        for d in (1, 2):
            pl.when(c >= d)(kv_copy(g, d).wait_recv)
        k_win = jnp.concatenate([kv[d, g, 0] for d in range(3)], axis=0)
        v_win = jnp.concatenate([kv[d, g, 1] for d in range(3)], axis=0)
        v_one = jnp.concatenate([v_win, jnp.full((3 * TOK, HD), -1.0, BF16)], axis=1)
        k_t[...] = k_win.T
        for j in range(PAIRS):
            p = g * PAIRS + j
            h = g * RATIO + 2 * j
            qp = qr[pl.ds(h, 2)].reshape(2 * TOK, HD)
            dp_in = doz[pl.ds(h, 2)].reshape(2 * TOK, 2 * HD)
            sc = dot_t(k_win, qp) * (SCALE * math.log2(math.e))
            b = bias[...]
            sc = sc + jnp.concatenate([b, b], axis=1)
            e = jnp.exp2(sc - jnp.max(sc, axis=0, keepdims=True))
            prob = e * (1.0 / jnp.sum(e, axis=0, keepdims=True))
            ds = (prob * dot_t(v_one, dp_in)).astype(BF16)
            p_win[:, 2 * j * TOK : 2 * (j + 1) * TOK] = prob.astype(BF16)
            ds_win[:, 2 * j * TOK : 2 * (j + 1) * TOK] = ds
            turned_grad = dot(k_t[...], ds)
            for i in range(2):
                x = turned_grad[:HALF, i * TOK : (i + 1) * TOK]
                y = turned_grad[HALF:, i * TOK : (i + 1) * TOK]
                grad = jnp.concatenate(
                    [x * tab_t[0] + y * tab_t[1], y * tab_t[0] - x * tab_t[1]], axis=0
                )
                dq[p, :, i * HD : (i + 1) * HD] = grad.T.astype(BF16)

            @pl.when(s >= 1)
            def _():
                if j == LONG:
                    pl.when(g < N_LONG)(long_copy(g).start)
                    pl.when(g >= N_LONG)(direct_copy(p).start)
                else:
                    direct_copy(p).start()

        dk = dot(ds_win[...], qr[pl.ds(g * RATIO, RATIO)].reshape(RATIO * TOK, HD))
        dv = dot(p_win[...], doz[pl.ds(g * RATIO, RATIO), :, 0:HD].reshape(RATIO * TOK, HD))
        own[g, 0] = dk[:TOK]
        own[g, 1] = dv[:TOK]
        for d in (1, 2):
            back_out[d - 1, g, 0] = dk[d * TOK : (d + 1) * TOK].astype(BF16)
            back_out[d - 1, g, 1] = dv[d * TOK : (d + 1) * TOK].astype(BF16)
            pl.when(c >= d)(back_copy(g, d).start)

        @pl.when((g >= 1) & (g <= N_LONG))
        def _():
            forward(g - 1)

        return carry

    lax.fori_loop(0, HK, group, 0)

    def finish(g, carry):
        for d in (1, 2):
            pl.when(c < n_ctx - d)(back_copy(g, d).wait_recv)
        dk = own[g, 0] + back_in[0, g, 0].astype(F32) + back_in[1, g, 0].astype(F32)
        dv = own[g, 1] + back_in[0, g, 1].astype(F32) + back_in[1, g, 1].astype(F32)
        dk = dk * SCALE
        cols = pl.ds(pl.multiple_of(g * HD, HD), HD)
        dk_ref[0, :, cols] = (dk * tab_c[...] - pltpu.roll(dk, HALF, 1) * tab_s[...]).astype(BF16)
        dv_ref[0, :, cols] = dv.astype(BF16)
        return carry

    lax.fori_loop(0, HK, finish, 0)

    def drain(g, carry):
        for d in (1, 2):
            pl.when(c < n_ctx - d)(kv_copy(g, d).wait_send)
            pl.when(c >= d)(back_copy(g, d).wait_send)

        @pl.when(s >= 1)
        def _():
            for j in range(PAIRS):
                direct_copy(g * PAIRS + j).wait_send()

        @pl.when((s == 0) & (g < N_LONG))
        def _():
            relay_copy(0, g, 1).wait_send()
            relay_copy(1, g, 2).wait_send()

        @pl.when((s == 2) & (g < N_LONG))
        def _():
            relay_copy(0, g, 0).wait_send()

        @pl.when(s <= 2)
        def _():
            for j in range(PAIRS):
                direct_copy(g * PAIRS + j).wait_recv()

        @pl.when(s == 3)
        def _():
            for j in range(PAIRS):
                zero_copy(g * PAIRS + j).wait()

        return carry

    lax.fori_loop(0, HK, drain, 0)


def hand_out(a, b, c, a_out, b_out, c_out, sem):
    copies = [
        pltpu.make_async_copy(b, b_out, sem.at[0]),
        pltpu.make_async_copy(c, c_out, sem.at[1]),
    ]
    for i in range(8):
        rows = pl.ds(i * (TOK // 8), TOK // 8)
        copies.append(pltpu.make_async_copy(a.at[0, rows], a_out.at[0, rows], sem.at[2 + i]))
    for copy in copies:
        copy.start()
    for copy in copies:
        copy.wait()


def solution(mesh):
    n_ctx = mesh.shape["ctx"]
    freq = np.broadcast_to(yarn_frequencies()[:, None], (HALF, TOK)).copy()

    def shards(q, k, v, o, do, doc_start, fetch_list):
        any_spec = pl.BlockSpec(memory_space=pl.ANY)
        hbm = pl.BlockSpec(memory_space=pltpu.HBM)
        vmem = pl.BlockSpec(memory_space=pltpu.VMEM)
        dma = pltpu.SemaphoreType.DMA
        results = pl.pallas_call(
            functools.partial(kernel, n_ctx),
            out_shape=(
                pltpu.VMEM((1, TOK, HQ * HD), BF16),
                pltpu.VMEM((1, TOK, HK * HD), BF16),
                pltpu.VMEM((1, TOK, HK * HD), BF16),
            ),
            in_specs=[hbm] * 8,
            out_specs=(vmem,) * 3,
            scratch_shapes=[
                pltpu.VMEM((1, TOK), jnp.int32),
                pltpu.VMEM((1, 2), jnp.int32),
                pltpu.VMEM((HALF, TOK), F32),
                pltpu.VMEM((TOK, HQ * HD), BF16),
                pltpu.VMEM((TOK, HK * HD), BF16),
                pltpu.VMEM((TOK, HQ * HD), BF16),
                pltpu.VMEM((TOK, HQ * HD), BF16),
                pltpu.VMEM((3, HK, 2, TOK, HD), BF16),
                pltpu.VMEM((HQ, TOK, HD), BF16),
                pltpu.VMEM((HQ, TOK, 2 * HD), BF16),
                pltpu.VMEM((3 * TOK, TOK), F32),
                pltpu.VMEM((2, HALF, TOK), F32),
                pltpu.VMEM((TOK, HD), F32),
                pltpu.VMEM((TOK, HD), F32),
                pltpu.VMEM((HD, 3 * TOK), BF16),
                pltpu.VMEM((3 * TOK, RATIO * TOK), BF16),
                pltpu.VMEM((3 * TOK, RATIO * TOK), BF16),
                pltpu.VMEM((HK, 2, TOK, HD), F32),
                pltpu.VMEM((2, HK, 2, TOK, HD), BF16),
                pltpu.VMEM((2, HK, 2, TOK, HD), BF16),
                pltpu.VMEM((HK * PAIRS, TOK, 2 * HD), BF16),
                pltpu.VMEM((2, HK, TOK, 2 * HD), BF16),
                dma((11,)),
                dma((2, HK)),
                dma((2, HK)),
                dma((2, HK)),
                dma((2, HK)),
                dma((HK * PAIRS,)),
                dma((HK * PAIRS,)),
                dma((2, HK)),
                dma((2, HK)),
            ],
            compiler_params=pltpu.CompilerParams(
                collective_id=0, has_side_effects=True, vmem_limit_bytes=28 << 20
            ),
            cost_estimate=pl.CostEstimate(flops=2_000_000_000, bytes_accessed=5_000_000, transcendentals=1_600_000),
        )(*(pltpu.with_memory_space_constraint(x, pltpu.HBM) for x in (doc_start.reshape(1, TOK), fetch_list, jnp.asarray(freq), q, k, v, o, do)))
        return pl.pallas_call(
            hand_out,
            out_shape=tuple(jax.ShapeDtypeStruct((1, TOK, n * HD), BF16) for n in (HQ, HK, HK)),
            in_specs=[vmem] * 3,
            out_specs=(hbm,) * 3,
            scratch_shapes=[dma((10,))],
            compiler_params=pltpu.CompilerParams(vmem_limit_bytes=1 << 20),
            cost_estimate=pl.CostEstimate(flops=0, bytes_accessed=2_600_000, transcendentals=0),
        )(*results)

    return jax.shard_map(
        shards,
        mesh=mesh,
        in_specs=(
            P("section", "ctx", None),
            P("section", "ctx", None),
            P("section", "ctx", None),
            P("section", "ctx", None),
            P("section", "ctx", None),
            P("ctx"),
            P("ctx", None),
        ),
        out_specs=(P("section", "ctx", None),) * 3,
        check_vma=False,
    )
```

```python
import functools
import math

import jax
import jax.numpy as jnp
import numpy as np
from jax import lax
from jax.experimental import pallas as pl
from jax.experimental.pallas import tpu as pltpu
from jax.sharding import PartitionSpec as P

HQ = 32
HK = 4
HD = 128
TOK = 128
RATIO = HQ // HK
PAIRS = RATIO // 2
HALF = HD // 2
ROPE_BASE = 1000000.0
TRAINED_CONTEXT = 32768.0
YARN_FACTOR = 4.0
NEG_LARGE = -1.0e30
SCALE = HD**-0.5
LONG = 0
N_LONG = 3
RELAY = 1
MESH = pl.DeviceIdType.MESH
F32 = jnp.float32
BF16 = jnp.bfloat16


def yarn_frequencies():
    def correction(rotations):
        return HD * math.log(TRAINED_CONTEXT / (rotations * 2.0 * math.pi)) / (2.0 * math.log(ROPE_BASE))

    lower = max(math.floor(correction(32.0)), 0)
    upper = min(math.ceil(correction(1.0)), HD - 1)
    spread = max(upper - lower, 0.001)
    index = np.arange(HALF, dtype=np.float64)
    base = ROPE_BASE ** (-2.0 * index / HD)
    ramp = np.clip((index - lower) / spread, 0.0, 1.0)
    return (base / YARN_FACTOR * ramp + base * (1.0 - ramp)).astype(np.float32)


def sin_cos(x):
    n = jnp.floor(x * (2.0 / math.pi) + 0.5)
    r = x - n * 1.5703125
    r = r - n * 4.83751296997070312e-4
    r = r - n * 7.54978995489188216e-8
    z = r * r
    sin = r + r * z * (-1.6666654611e-1 + z * (8.3321608736e-3 + z * -1.9515295891e-4))
    cos = 1.0 - 0.5 * z + z * z * (4.166664568298827e-2 + z * (-1.388731625493765e-3 + z * 2.443315711809948e-5))
    q = n.astype(jnp.int32) & 3
    odd = (q & 1) == 1
    s = jnp.where(odd, cos, sin)
    c = jnp.where(odd, sin, cos)
    return jnp.where(q >= 2, -s, s), jnp.where((q == 1) | (q == 2), -c, c)


def dot_t(a, b):
    return lax.dot_general(a, b, (((1,), (1,)), ((), ())), preferred_element_type=F32)


def dot(a, b):
    return jnp.dot(a, b, preferred_element_type=F32)


def kernel(
    n_ctx,
    doc_hbm, fetch_hbm, freq_hbm, q_hbm, k_hbm, v_hbm, o_hbm, do_hbm,
    out_ref, dk_ref, dv_ref,
    doc_ref, fetch_ref, freq_ref, q_in, o_in, do_in,
    kv, qr, doz, bias, tab_t, tab_c, tab_s, k_t, p_win, ds_win, own, back_out, back_in, dq, relay,
    ready, small_sem, kv_sem, query_sem, kv_send, kv_recv, back_send, back_recv, dq_send, out_recv, relay_recv, relay_send,
):
    c = lax.axis_index("ctx")
    s = lax.axis_index("section")

    small = [
        pltpu.make_async_copy(doc_hbm, doc_ref, small_sem.at[0]),
        pltpu.make_async_copy(freq_hbm, freq_ref, small_sem.at[1]),
        pltpu.make_async_copy(fetch_hbm, fetch_ref, small_sem.at[2]),
    ]

    def head_cols(ref, g):
        return ref.at[0, :, pl.ds(pl.multiple_of(g * HD, HD), HD)]

    def kv_loads(g):
        return [
            pltpu.make_async_copy(head_cols(x, g), kv.at[0, g, i], kv_sem.at[i, g]) for i, x in enumerate((k_hbm, v_hbm))
        ]

    def query_loads(g):
        cols = pl.ds(pl.multiple_of(g * RATIO * HD, RATIO * HD), RATIO * HD)
        return [
            pltpu.make_async_copy(x.at[0, :, cols], y.at[g], query_sem.at[i, g])
            for i, (x, y) in enumerate(((q_hbm, q_in), (do_hbm, do_in), (o_hbm, o_in)))
        ]

    for load in small:
        load.start()
    for g in range(HK):
        for load in kv_loads(g) + query_loads(g):
            load.start()

    barrier = pltpu.get_barrier_semaphore()
    for d in (1, 2):
        @pl.when(c >= d)
        def _():
            pl.semaphore_signal(barrier, inc=1, device_id=(c - d, s), device_id_type=MESH)
    for me, others in ((0, (1, 2, 3)), (1, (2,)), (2, (3,))):
        @pl.when(s == me)
        def _():
            for other in others:
                pl.semaphore_signal(barrier, inc=1, device_id=(c, other), device_id_type=MESH)

    greeted = s - s // 3 + (c < n_ctx - 1).astype(jnp.int32) + (c < n_ctx - 2).astype(jnp.int32)

    @pl.when(greeted > 0)
    def _():
        pl.semaphore_wait(barrier, greeted)

    for me, others in ((1, (0,)), (2, (0, 1))):
        @pl.when(s == me)
        def _():
            for other in others:
                pl.semaphore_signal(ready, inc=1, device_id=(c, other), device_id_type=MESH)

    def kv_copies(g, d):
        return [
            pltpu.make_async_remote_copy(
                src_ref=head_cols(x, g), dst_ref=kv.at[d, g, i],
                send_sem=kv_send.at[d - 1, g, i], recv_sem=kv_recv.at[d - 1, g, i],
                device_id=(c + d, s), device_id_type=MESH,
            )
            for i, x in enumerate((k_hbm, v_hbm))
        ]

    for g in range(1):
        for d in (1, 2):
            @pl.when(c < n_ctx - d)
            def _():
                for copy in kv_copies(g, d):
                    copy.start()
    for d in (1, 2):
        @pl.when(c < d)
        def _():
            kv[d] = jnp.zeros((HK, 2, TOK, HD), BF16)
        @pl.when(c >= n_ctx - d)
        def _():
            back_in[d - 1] = jnp.zeros((HK, 2, TOK, HD), BF16)

    for load in small:
        load.wait()
    first = c * TOK
    lane = lax.broadcasted_iota(jnp.int32, (1, TOK), 1)
    lane_t = lane + first
    start = doc_ref[...]
    factor = 0.1 * math.log(YARN_FACTOR) + 1.0
    low = lax.broadcasted_iota(jnp.int32, (TOK, HD), 1) < HALF
    for d in range(3):
        position = lane_t - start if d == 0 else jnp.maximum(lane_t - d * TOK - start[:, 0:1], 0)
        sin, cos = sin_cos(position.astype(F32) * freq_ref[...])
        sin = sin * factor
        cos = cos * factor
        if d == 0:
            tab_t[0] = cos * SCALE
            tab_t[1] = sin * SCALE
        turned = jnp.concatenate([cos, sin], axis=0).T
        swapped = pltpu.roll(turned, HALF, 1)
        tab_c[d] = jnp.where(low, turned, swapped)
        tab_s[d] = jnp.where(low, -swapped, turned)

    def rope(x, d):
        x = x.astype(F32)
        return (x * tab_c[d] + pltpu.roll(x, HALF, 1) * tab_s[d]).astype(BF16)

    def zero_copy(p):
        return pltpu.make_async_copy(
            relay.at[0, 0], out_ref.at[0, :, pl.ds(pl.multiple_of(p * 2 * HD, 2 * HD), 2 * HD)], out_recv.at[p]
        )

    @pl.when(s == 3)
    def _():
        relay[0, 0] = jnp.zeros((TOK, 2 * HD), BF16)

        def put(p, carry):
            zero_copy(p).start()
            return carry

        lax.fori_loop(0, HK * PAIRS, put, 0)

    row = lax.broadcasted_iota(jnp.int32, (TOK, TOK), 0)
    for d in range(3):
        u = first - d * TOK + row
        allowed = (u >= start) & (u <= lane_t)
        if d > 0:
            allowed = allowed & (fetch_ref[:, d - 1 : d] == 1)
        bias[d * TOK : (d + 1) * TOK, :] = jnp.where(allowed, 0.0, NEG_LARGE)

    for g in range(HK):
        for load in query_loads(g) + kv_loads(g):
            load.wait()

    def prepare(g):
        for i in range(RATIO):
            h = g * RATIO + i
            cols = slice(i * HD, (i + 1) * HD)
            qr[h] = rope(q_in[g, :, cols], 0)
            grad = do_in[g, :, cols]
            prod = grad.astype(F32) * o_in[g, :, cols].astype(F32)
            prod = prod + pltpu.roll(prod, HALF, 1)
            high = prod.astype(BF16).astype(F32)
            doz[h, :, 0:HD] = grad
            doz[h, :, HD : 2 * HD] = jnp.where(low, high, prod - high).astype(BF16)

    lax.fori_loop(0, HK, lambda g, c: (prepare(g), c)[1], 0)

    for g in range(1, HK):
        for d in (1, 2):
            @pl.when(c < n_ctx - d)
            def _():
                for copy in kv_copies(g, d):
                    copy.start()

    def out_cols(p):
        return out_ref.at[0, :, pl.ds(pl.multiple_of(p * 2 * HD, 2 * HD), 2 * HD)]

    def direct_copy(p):
        return pltpu.make_async_remote_copy(
            src_ref=dq.at[p], dst_ref=out_cols(p), send_sem=dq_send.at[p], recv_sem=out_recv.at[p],
            device_id=(c, s - 1), device_id_type=MESH,
        )

    def long_copy(g):
        return pltpu.make_async_remote_copy(
            src_ref=dq.at[g * PAIRS + LONG], dst_ref=relay.at[s // 3, g],
            send_sem=dq_send.at[g * PAIRS + LONG], recv_sem=relay_recv.at[s // 3, g],
            device_id=(c, 2 * (1 - s // 2)), device_id_type=MESH,
        )

    def relay_copy(slot, g, target):
        p = g * PAIRS + LONG
        return pltpu.make_async_remote_copy(
            src_ref=relay.at[slot, g], dst_ref=out_cols(p),
            send_sem=relay_send.at[slot, g], recv_sem=out_recv.at[p],
            device_id=(c, target), device_id_type=MESH,
        )

    def arrival(slot, g):
        return pltpu.make_async_remote_copy(
            src_ref=dq.at[g * PAIRS + LONG], dst_ref=relay.at[slot, g],
            send_sem=dq_send.at[g * PAIRS + LONG], recv_sem=relay_recv.at[slot, g],
            device_id=(c, 0), device_id_type=MESH,
        )

    def forward(g):
        @pl.when(s == 0)
        def _():
            @pl.when(g == 0)
            def _():
                pl.semaphore_wait(ready, 2)

            arrival(0, g).wait_recv()
            relay_copy(0, g, 1).start()
            arrival(1, g).wait_recv()
            relay_copy(1, g, 2).start()

        @pl.when(s == 2)
        def _():
            arrival(0, g).wait_recv()
            relay_copy(0, g, 0).start()

    def back_copy(g, d):
        return pltpu.make_async_remote_copy(
            src_ref=back_out.at[d - 1, g], dst_ref=back_in.at[d - 1, g],
            send_sem=back_send.at[d - 1, g], recv_sem=back_recv.at[d - 1, g],
            device_id=(c - d, s), device_id_type=MESH,
        )

    def group(g, carry):
        for d in (1, 2):
            @pl.when(c >= d)
            def _():
                for copy in kv_copies(g, d):
                    copy.wait_recv()

        k_win = jnp.concatenate([rope(kv[d, g, 0], d) for d in range(3)], axis=0)
        v_win = jnp.concatenate([kv[d, g, 1] for d in range(3)], axis=0)
        v_one = jnp.concatenate([v_win, jnp.full((3 * TOK, HD), -1.0, BF16)], axis=1)
        k_t[...] = k_win.T
        for j in range(PAIRS):
            p = g * PAIRS + j
            h = g * RATIO + 2 * j
            qp = qr[pl.ds(h, 2)].reshape(2 * TOK, HD)
            dp_in = doz[pl.ds(h, 2)].reshape(2 * TOK, 2 * HD)
            sc = dot_t(k_win, qp) * (SCALE * math.log2(math.e))
            b = bias[...]
            sc = sc + jnp.concatenate([b, b], axis=1)
            e = jnp.exp2(sc - jnp.max(sc, axis=0, keepdims=True))
            prob = e * (1.0 / jnp.sum(e, axis=0, keepdims=True))
            ds = (prob * dot_t(v_one, dp_in)).astype(BF16)
            p_win[:, 2 * j * TOK : 2 * (j + 1) * TOK] = prob.astype(BF16)
            ds_win[:, 2 * j * TOK : 2 * (j + 1) * TOK] = ds
            turned_grad = dot(k_t[...], ds)
            for i in range(2):
                x = turned_grad[:HALF, i * TOK : (i + 1) * TOK]
                y = turned_grad[HALF:, i * TOK : (i + 1) * TOK]
                grad = jnp.concatenate(
                    [x * tab_t[0] + y * tab_t[1], y * tab_t[0] - x * tab_t[1]], axis=0
                )
                dq[p, :, i * HD : (i + 1) * HD] = grad.T.astype(BF16)

            if j == LONG:
                @pl.when((s == 1) & (g == 0))
                def _():
                    pl.semaphore_wait(ready, 1)

            @pl.when(s >= 1)
            def _():
                if j == LONG:
                    pl.when(g < N_LONG)(long_copy(g).start)
                    pl.when(g >= N_LONG)(direct_copy(p).start)
                else:
                    direct_copy(p).start()

        dk = dot(ds_win[...], qr[pl.ds(g * RATIO, RATIO)].reshape(RATIO * TOK, HD))
        dv = dot(p_win[...], doz[pl.ds(g * RATIO, RATIO), :, 0:HD].reshape(RATIO * TOK, HD))
        own[g, 0] = dk[:TOK]
        own[g, 1] = dv[:TOK]
        for d in (1, 2):
            back_out[d - 1, g, 0] = dk[d * TOK : (d + 1) * TOK].astype(BF16)
            back_out[d - 1, g, 1] = dv[d * TOK : (d + 1) * TOK].astype(BF16)
            pl.when(c >= d)(back_copy(g, d).start)

        @pl.when((g >= 1) & (g <= N_LONG))
        def _():
            forward(g - 1)

        return carry

    lax.fori_loop(0, HK, group, 0)

    def finish(g, carry):
        for d in (1, 2):
            pl.when(c < n_ctx - d)(back_copy(g, d).wait_recv)
        dk = own[g, 0] + back_in[0, g, 0].astype(F32) + back_in[1, g, 0].astype(F32)
        dv = own[g, 1] + back_in[0, g, 1].astype(F32) + back_in[1, g, 1].astype(F32)
        dk = dk * SCALE
        cols = pl.ds(pl.multiple_of(g * HD, HD), HD)
        dk_ref[0, :, cols] = (dk * tab_c[0] - pltpu.roll(dk, HALF, 1) * tab_s[0]).astype(BF16)
        dv_ref[0, :, cols] = dv.astype(BF16)
        return carry

    lax.fori_loop(0, HK, finish, 0)

    def drain(g, carry):
        for d in (1, 2):
            @pl.when(c < n_ctx - d)
            def _():
                for copy in kv_copies(g, d):
                    copy.wait_send()

            pl.when(c >= d)(back_copy(g, d).wait_send)

        @pl.when(s >= 1)
        def _():
            for j in range(PAIRS):
                direct_copy(g * PAIRS + j).wait_send()

        @pl.when((s == 0) & (g < N_LONG))
        def _():
            relay_copy(0, g, 1).wait_send()
            relay_copy(1, g, 2).wait_send()

        @pl.when((s == 2) & (g < N_LONG))
        def _():
            relay_copy(0, g, 0).wait_send()

        @pl.when(s <= 2)
        def _():
            for j in range(PAIRS):
                direct_copy(g * PAIRS + j).wait_recv()

        @pl.when(s == 3)
        def _():
            for j in range(PAIRS):
                zero_copy(g * PAIRS + j).wait()

        return carry

    lax.fori_loop(0, HK, drain, 0)


def hand_out(a, b, c, a_out, b_out, c_out, sem):
    copies = [
        pltpu.make_async_copy(b, b_out, sem.at[0]),
        pltpu.make_async_copy(c, c_out, sem.at[1]),
    ]
    for i in range(8):
        rows = pl.ds(i * (TOK // 8), TOK // 8)
        copies.append(pltpu.make_async_copy(a.at[0, rows], a_out.at[0, rows], sem.at[2 + i]))
    for copy in copies:
        copy.start()
    for copy in copies:
        copy.wait()


def solution(mesh):
    n_ctx = mesh.shape["ctx"]
    freq = np.broadcast_to(yarn_frequencies()[:, None], (HALF, TOK)).copy()

    def shards(q, k, v, o, do, doc_start, fetch_list):
        any_spec = pl.BlockSpec(memory_space=pl.ANY)
        hbm = pl.BlockSpec(memory_space=pltpu.HBM)
        vmem = pl.BlockSpec(memory_space=pltpu.VMEM)
        dma = pltpu.SemaphoreType.DMA
        results = pl.pallas_call(
            functools.partial(kernel, n_ctx),
            out_shape=(
                pltpu.VMEM((1, TOK, HQ * HD), BF16),
                pltpu.VMEM((1, TOK, HK * HD), BF16),
                pltpu.VMEM((1, TOK, HK * HD), BF16),
            ),
            in_specs=[hbm] * 8,
            out_specs=(vmem,) * 3,
            scratch_shapes=[
                pltpu.VMEM((1, TOK), jnp.int32),
                pltpu.VMEM((1, 2), jnp.int32),
                pltpu.VMEM((HALF, TOK), F32),
                pltpu.VMEM((HK, TOK, RATIO * HD), BF16),
                pltpu.VMEM((HK, TOK, RATIO * HD), BF16),
                pltpu.VMEM((HK, TOK, RATIO * HD), BF16),
                pltpu.VMEM((3, HK, 2, TOK, HD), BF16),
                pltpu.VMEM((HQ, TOK, HD), BF16),
                pltpu.VMEM((HQ, TOK, 2 * HD), BF16),
                pltpu.VMEM((3 * TOK, TOK), F32),
                pltpu.VMEM((2, HALF, TOK), F32),
                pltpu.VMEM((3, TOK, HD), F32),
                pltpu.VMEM((3, TOK, HD), F32),
                pltpu.VMEM((HD, 3 * TOK), BF16),
                pltpu.VMEM((3 * TOK, RATIO * TOK), BF16),
                pltpu.VMEM((3 * TOK, RATIO * TOK), BF16),
                pltpu.VMEM((HK, 2, TOK, HD), F32),
                pltpu.VMEM((2, HK, 2, TOK, HD), BF16),
                pltpu.VMEM((2, HK, 2, TOK, HD), BF16),
                pltpu.VMEM((HK * PAIRS, TOK, 2 * HD), BF16),
                pltpu.VMEM((2, HK, TOK, 2 * HD), BF16),
                pltpu.SemaphoreType.REGULAR,
                dma((3,)),
                dma((2, HK)),
                dma((3, HK)),
                dma((2, HK, 2)),
                dma((2, HK, 2)),
                dma((2, HK)),
                dma((2, HK)),
                dma((HK * PAIRS,)),
                dma((HK * PAIRS,)),
                dma((2, HK)),
                dma((2, HK)),
            ],
            compiler_params=pltpu.CompilerParams(
                collective_id=0, has_side_effects=True, vmem_limit_bytes=28 << 20
            ),
            cost_estimate=pl.CostEstimate(flops=2_000_000_000, bytes_accessed=5_000_000, transcendentals=1_600_000),
        )(*(pltpu.with_memory_space_constraint(x, pltpu.HBM) for x in (doc_start.reshape(1, TOK), fetch_list, jnp.asarray(freq), q, k, v, o, do)))
        return pl.pallas_call(
            hand_out,
            out_shape=tuple(jax.ShapeDtypeStruct((1, TOK, n * HD), BF16) for n in (HQ, HK, HK)),
            in_specs=[vmem] * 3,
            out_specs=(hbm,) * 3,
            scratch_shapes=[dma((10,))],
            compiler_params=pltpu.CompilerParams(vmem_limit_bytes=1 << 20),
            cost_estimate=pl.CostEstimate(flops=0, bytes_accessed=2_600_000, transcendentals=0),
        )(*results)

    return jax.shard_map(
        shards,
        mesh=mesh,
        in_specs=(
            P("section", "ctx", None),
            P("section", "ctx", None),
            P("section", "ctx", None),
            P("section", "ctx", None),
            P("section", "ctx", None),
            P("ctx"),
            P("ctx", None),
        ),
        out_specs=(P("section", "ctx", None),) * 3,
        check_vma=False,
    )
```

```python
import functools
import math

import jax
import jax.numpy as jnp
import numpy as np
from jax import lax
from jax.experimental import pallas as pl
from jax.experimental.pallas import tpu as pltpu
from jax.sharding import PartitionSpec as P

HQ = 32
HK = 4
HD = 128
TOK = 128
RATIO = HQ // HK
PAIRS = RATIO // 2
HALF = HD // 2
ROPE_BASE = 1000000.0
TRAINED_CONTEXT = 32768.0
YARN_FACTOR = 4.0
NEG_LARGE = -1.0e30
SCALE = HD**-0.5
LONG = 1
N_LONG = 3
CHAIN = 16
SIDE = (6, 10)
RELAY = 1
MESH = pl.DeviceIdType.MESH
F32 = jnp.float32
BF16 = jnp.bfloat16


def yarn_frequencies():
    def correction(rotations):
        return HD * math.log(TRAINED_CONTEXT / (rotations * 2.0 * math.pi)) / (2.0 * math.log(ROPE_BASE))

    lower = max(math.floor(correction(32.0)), 0)
    upper = min(math.ceil(correction(1.0)), HD - 1)
    spread = max(upper - lower, 0.001)
    index = np.arange(HALF, dtype=np.float64)
    base = ROPE_BASE ** (-2.0 * index / HD)
    ramp = np.clip((index - lower) / spread, 0.0, 1.0)
    return (base / YARN_FACTOR * ramp + base * (1.0 - ramp)).astype(np.float32)


def sin_cos(x):
    n = jnp.floor(x * (2.0 / math.pi) + 0.5)
    r = x - n * 1.5703125
    r = r - n * 4.83751296997070312e-4
    r = r - n * 7.54978995489188216e-8
    z = r * r
    sin = r + r * z * (-1.6666654611e-1 + z * (8.3321608736e-3 + z * -1.9515295891e-4))
    cos = 1.0 - 0.5 * z + z * z * (4.166664568298827e-2 + z * (-1.388731625493765e-3 + z * 2.443315711809948e-5))
    q = n.astype(jnp.int32) & 3
    odd = (q & 1) == 1
    s = jnp.where(odd, cos, sin)
    c = jnp.where(odd, sin, cos)
    return jnp.where(q >= 2, -s, s), jnp.where((q == 1) | (q == 2), -c, c)


def dot_t(a, b):
    return lax.dot_general(a, b, (((1,), (1,)), ((), ())), preferred_element_type=F32)


def dot(a, b):
    return jnp.dot(a, b, preferred_element_type=F32)


def kernel(
    n_ctx,
    doc_hbm, fetch_hbm, freq_hbm, q_hbm, k_hbm, v_hbm, o_hbm, do_hbm,
    out_ref, dk_ref, dv_ref,
    doc_ref, fetch_ref, freq_ref, q_in, o_in, do_in,
    kv, qr, doz, bias, tab_t, tab_c, tab_s, k_t, p_win, ds_win, own, back_out, back_in, dq, relay, side,
    ready, helped, small_sem, kv_sem, query_sem, kv_send, kv_recv, back_send, back_recv, dq_send, out_recv, relay_recv, relay_send, side_recv, side_send,
):
    c = lax.axis_index("ctx")
    s = lax.axis_index("section")

    place = lax.rem(c, CHAIN)
    first_chip = (place < 2) & (s >= 1)
    helps = [(place // 2 == i + 1) & (s <= 2) for i in range(len(SIDE))]

    small = [
        pltpu.make_async_copy(doc_hbm, doc_ref, small_sem.at[0]),
        pltpu.make_async_copy(freq_hbm, freq_ref, small_sem.at[1]),
        pltpu.make_async_copy(fetch_hbm, fetch_ref, small_sem.at[2]),
    ]

    def head_cols(ref, g):
        return ref.at[0, :, pl.ds(pl.multiple_of(g * HD, HD), HD)]

    def kv_loads(g):
        return [
            pltpu.make_async_copy(head_cols(x, g), kv.at[0, g, i], kv_sem.at[i, g]) for i, x in enumerate((k_hbm, v_hbm))
        ]

    def query_loads(g):
        cols = pl.ds(pl.multiple_of(g * RATIO * HD, RATIO * HD), RATIO * HD)
        return [
            pltpu.make_async_copy(x.at[0, :, cols], y.at[g], query_sem.at[i, g])
            for i, (x, y) in enumerate(((q_hbm, q_in), (do_hbm, do_in), (o_hbm, o_in)))
        ]

    for load in small:
        load.start()
    for g in range(HK):
        for load in kv_loads(g) + query_loads(g):
            load.start()

    barrier = pltpu.get_barrier_semaphore()
    for d in (1, 2):
        @pl.when(c >= d)
        def _():
            pl.semaphore_signal(barrier, inc=1, device_id=(c - d, s), device_id_type=MESH)
    for me, others in ((0, (1, 2, 3)), (1, (2,)), (2, (3,))):
        @pl.when(s == me)
        def _():
            for other in others:
                pl.semaphore_signal(barrier, inc=1, device_id=(c, other), device_id_type=MESH)

    @pl.when(first_chip)
    def _():
        for i in range(len(SIDE)):
            pl.semaphore_signal(barrier, inc=1, device_id=(c + 2 * i + 2, s - 1), device_id_type=MESH)

    greeted = s - s // 3 + sum(h.astype(jnp.int32) for h in helps) + (c < n_ctx - 1).astype(jnp.int32) + (c < n_ctx - 2).astype(jnp.int32)

    @pl.when(greeted > 0)
    def _():
        pl.semaphore_wait(barrier, greeted)

    for me, others in ((1, (0,)), (2, (0, 1))):
        @pl.when(s == me)
        def _():
            for other in others:
                pl.semaphore_signal(ready, inc=1, device_id=(c, other), device_id_type=MESH)

    for i in range(len(SIDE)):
        @pl.when(helps[i])
        def _():
            pl.semaphore_signal(helped, inc=1, device_id=(c - 2 * i - 2, s + 1), device_id_type=MESH)

    def kv_copies(g, d):
        return [
            pltpu.make_async_remote_copy(
                src_ref=head_cols(x, g), dst_ref=kv.at[d, g, i],
                send_sem=kv_send.at[d - 1, g, i], recv_sem=kv_recv.at[d - 1, g, i],
                device_id=(c + d, s), device_id_type=MESH,
            )
            for i, x in enumerate((k_hbm, v_hbm))
        ]

    for g in range(1):
        for d in (1, 2):
            @pl.when(c < n_ctx - d)
            def _():
                for copy in kv_copies(g, d):
                    copy.start()
    for d in (1, 2):
        @pl.when(c < d)
        def _():
            kv[d] = jnp.zeros((HK, 2, TOK, HD), BF16)
        @pl.when(c >= n_ctx - d)
        def _():
            back_in[d - 1] = jnp.zeros((HK, 2, TOK, HD), BF16)

    for load in small:
        load.wait()
    first = c * TOK
    lane = lax.broadcasted_iota(jnp.int32, (1, TOK), 1)
    lane_t = lane + first
    start = doc_ref[...]
    factor = 0.1 * math.log(YARN_FACTOR) + 1.0
    low = lax.broadcasted_iota(jnp.int32, (TOK, HD), 1) < HALF
    for d in range(3):
        position = lane_t - start if d == 0 else jnp.maximum(lane_t - d * TOK - start[:, 0:1], 0)
        sin, cos = sin_cos(position.astype(F32) * freq_ref[...])
        sin = sin * factor
        cos = cos * factor
        if d == 0:
            tab_t[0] = cos * SCALE
            tab_t[1] = sin * SCALE
        turned = jnp.concatenate([cos, sin], axis=0).T
        swapped = pltpu.roll(turned, HALF, 1)
        tab_c[d] = jnp.where(low, turned, swapped)
        tab_s[d] = jnp.where(low, -swapped, turned)

    def rope(x, d):
        x = x.astype(F32)
        return (x * tab_c[d] + pltpu.roll(x, HALF, 1) * tab_s[d]).astype(BF16)

    def zero_copy(p):
        return pltpu.make_async_copy(
            relay.at[0, 0], out_ref.at[0, :, pl.ds(pl.multiple_of(p * 2 * HD, 2 * HD), 2 * HD)], out_recv.at[p]
        )

    @pl.when(s == 3)
    def _():
        relay[0, 0] = jnp.zeros((TOK, 2 * HD), BF16)

        def put(p, carry):
            zero_copy(p).start()
            return carry

        lax.fori_loop(0, HK * PAIRS, put, 0)

    row = lax.broadcasted_iota(jnp.int32, (TOK, TOK), 0)
    for d in range(3):
        u = first - d * TOK + row
        allowed = (u >= start) & (u <= lane_t)
        if d > 0:
            allowed = allowed & (fetch_ref[:, d - 1 : d] == 1)
        bias[d * TOK : (d + 1) * TOK, :] = jnp.where(allowed, 0.0, NEG_LARGE)

    for g in range(HK):
        for load in query_loads(g) + kv_loads(g):
            load.wait()

    def prepare(g):
        for i in range(RATIO):
            h = g * RATIO + i
            cols = slice(i * HD, (i + 1) * HD)
            qr[h] = rope(q_in[g, :, cols], 0)
            grad = do_in[g, :, cols]
            prod = grad.astype(F32) * o_in[g, :, cols].astype(F32)
            prod = prod + pltpu.roll(prod, HALF, 1)
            high = prod.astype(BF16).astype(F32)
            doz[h, :, 0:HD] = grad
            doz[h, :, HD : 2 * HD] = jnp.where(low, high, prod - high).astype(BF16)

    lax.fori_loop(0, HK, lambda g, c: (prepare(g), c)[1], 0)

    for g in range(1, HK):
        for d in (1, 2):
            @pl.when(c < n_ctx - d)
            def _():
                for copy in kv_copies(g, d):
                    copy.start()

    def out_cols(p):
        return out_ref.at[0, :, pl.ds(pl.multiple_of(p * 2 * HD, 2 * HD), 2 * HD)]

    def direct_copy(p):
        return pltpu.make_async_remote_copy(
            src_ref=dq.at[p], dst_ref=out_cols(p), send_sem=dq_send.at[p], recv_sem=out_recv.at[p],
            device_id=(c, s - 1), device_id_type=MESH,
        )

    def long_copy(g):
        return pltpu.make_async_remote_copy(
            src_ref=dq.at[g * PAIRS + LONG], dst_ref=relay.at[s // 3, g],
            send_sem=dq_send.at[g * PAIRS + LONG], recv_sem=relay_recv.at[s // 3, g],
            device_id=(c, 2 * (1 - s // 2)), device_id_type=MESH,
        )

    def side_copy(i):
        return pltpu.make_async_remote_copy(
            src_ref=dq.at[SIDE[i]], dst_ref=side.at[i],
            send_sem=dq_send.at[SIDE[i]], recv_sem=side_recv.at[i],
            device_id=(c + 2 * i + 2, s - 1), device_id_type=MESH,
        )

    def side_back(i):
        return pltpu.make_async_remote_copy(
            src_ref=side.at[i], dst_ref=out_cols(SIDE[i]),
            send_sem=side_send.at[i], recv_sem=out_recv.at[SIDE[i]],
            device_id=(c - 2 * i - 2, s), device_id_type=MESH,
        )

    def relay_copy(slot, g, target):
        p = g * PAIRS + LONG
        return pltpu.make_async_remote_copy(
            src_ref=relay.at[slot, g], dst_ref=out_cols(p),
            send_sem=relay_send.at[slot, g], recv_sem=out_recv.at[p],
            device_id=(c, target), device_id_type=MESH,
        )

    def arrival(slot, g):
        return pltpu.make_async_remote_copy(
            src_ref=dq.at[g * PAIRS + LONG], dst_ref=relay.at[slot, g],
            send_sem=dq_send.at[g * PAIRS + LONG], recv_sem=relay_recv.at[slot, g],
            device_id=(c, 0), device_id_type=MESH,
        )

    def forward(g):
        @pl.when(s == 0)
        def _():
            @pl.when(g == 0)
            def _():
                pl.semaphore_wait(ready, 2)

            arrival(0, g).wait_recv()
            relay_copy(0, g, 1).start()
            arrival(1, g).wait_recv()
            relay_copy(1, g, 2).start()

        @pl.when(s == 2)
        def _():
            arrival(0, g).wait_recv()
            relay_copy(0, g, 0).start()

    def back_copy(g, d):
        return pltpu.make_async_remote_copy(
            src_ref=back_out.at[d - 1, g], dst_ref=back_in.at[d - 1, g],
            send_sem=back_send.at[d - 1, g], recv_sem=back_recv.at[d - 1, g],
            device_id=(c - d, s), device_id_type=MESH,
        )

    def group(g, carry):
        for d in (1, 2):
            @pl.when(c >= d)
            def _():
                for copy in kv_copies(g, d):
                    copy.wait_recv()

        k_win = jnp.concatenate([rope(kv[d, g, 0], d) for d in range(3)], axis=0)
        v_win = jnp.concatenate([kv[d, g, 1] for d in range(3)], axis=0)
        v_one = jnp.concatenate([v_win, jnp.full((3 * TOK, HD), -1.0, BF16)], axis=1)
        k_t[...] = k_win.T
        for j in range(PAIRS):
            p = g * PAIRS + j
            h = g * RATIO + 2 * j
            qp = qr[pl.ds(h, 2)].reshape(2 * TOK, HD)
            dp_in = doz[pl.ds(h, 2)].reshape(2 * TOK, 2 * HD)
            sc = dot_t(k_win, qp) * (SCALE * math.log2(math.e))
            b = bias[...]
            sc = sc + jnp.concatenate([b, b], axis=1)
            e = jnp.exp2(sc - jnp.max(sc, axis=0, keepdims=True))
            prob = e * (1.0 / jnp.sum(e, axis=0, keepdims=True))
            ds = (prob * dot_t(v_one, dp_in)).astype(BF16)
            p_win[:, 2 * j * TOK : 2 * (j + 1) * TOK] = prob.astype(BF16)
            ds_win[:, 2 * j * TOK : 2 * (j + 1) * TOK] = ds
            if j == 0:
                @pl.when(first_chip & (g == 1))
                def _():
                    pl.semaphore_wait(helped, len(SIDE))

            if j == LONG:
                @pl.when((s == 1) & (g == 0))
                def _():
                    pl.semaphore_wait(ready, 1)

            @pl.when(s >= 1)
            def _():
                turned_grad = dot(k_t[...], ds_win[:, 2 * j * TOK : 2 * (j + 1) * TOK])
                for i in range(2):
                    x = turned_grad[:HALF, i * TOK : (i + 1) * TOK]
                    y = turned_grad[HALF:, i * TOK : (i + 1) * TOK]
                    grad = jnp.concatenate(
                        [x * tab_t[0] + y * tab_t[1], y * tab_t[0] - x * tab_t[1]], axis=0
                    )
                    dq[p, :, i * HD : (i + 1) * HD] = grad.T.astype(BF16)
                if j == LONG:
                    pl.when(g < N_LONG)(long_copy(g).start)
                    pl.when(g >= N_LONG)(direct_copy(p).start)
                elif j == 2:
                    aside = first_chip & ((g == 1) | (g == 2))
                    for i in range(len(SIDE)):
                        pl.when(first_chip & (p == SIDE[i]))(side_copy(i).start)
                    pl.when((g < 3) & jnp.logical_not(aside))(direct_copy(p).start)
                elif j == 3:
                    pl.when(g < 2)(direct_copy(p).start)
                else:
                    direct_copy(p).start()

        dk = dot(ds_win[...], qr[pl.ds(g * RATIO, RATIO)].reshape(RATIO * TOK, HD))
        dv = dot(p_win[...], doz[pl.ds(g * RATIO, RATIO), :, 0:HD].reshape(RATIO * TOK, HD))
        own[g, 0] = dk[:TOK]
        own[g, 1] = dv[:TOK]
        for d in (1, 2):
            back_out[d - 1, g, 0] = dk[d * TOK : (d + 1) * TOK].astype(BF16)
            back_out[d - 1, g, 1] = dv[d * TOK : (d + 1) * TOK].astype(BF16)
            pl.when(c >= d)(back_copy(g, d).start)

        @pl.when((g >= 1) & (g <= N_LONG) & (s == 2))
        def _():
            forward(g - 1)

        return carry

    lax.fori_loop(0, HK, group, 0)

    @pl.when(s == 0)
    def _():
        for g in range(N_LONG):
            forward(g)

    @pl.when(s >= 1)
    def _():
        for p in (11, 14, 15):
            direct_copy(p).start()

    for i in range(len(SIDE)):
        @pl.when(helps[i])
        def _():
            side_copy(i).wait_recv()
            side_back(i).start()


    def finish(g, carry):
        for d in (1, 2):
            pl.when(c < n_ctx - d)(back_copy(g, d).wait_recv)
        dk = own[g, 0] + back_in[0, g, 0].astype(F32) + back_in[1, g, 0].astype(F32)
        dv = own[g, 1] + back_in[0, g, 1].astype(F32) + back_in[1, g, 1].astype(F32)
        dk = dk * SCALE
        cols = pl.ds(pl.multiple_of(g * HD, HD), HD)
        dk_ref[0, :, cols] = (dk * tab_c[0] - pltpu.roll(dk, HALF, 1) * tab_s[0]).astype(BF16)
        dv_ref[0, :, cols] = dv.astype(BF16)
        return carry

    lax.fori_loop(0, HK, finish, 0)

    def drain(g, carry):
        for d in (1, 2):
            @pl.when(c < n_ctx - d)
            def _():
                for copy in kv_copies(g, d):
                    copy.wait_send()

            pl.when(c >= d)(back_copy(g, d).wait_send)

        @pl.when(s >= 1)
        def _():
            for j in range(PAIRS):
                direct_copy(g * PAIRS + j).wait_send()

        @pl.when((s == 0) & (g < N_LONG))
        def _():
            relay_copy(0, g, 1).wait_send()
            relay_copy(1, g, 2).wait_send()

        @pl.when((s == 2) & (g < N_LONG))
        def _():
            relay_copy(0, g, 0).wait_send()

        @pl.when(s <= 2)
        def _():
            for j in range(PAIRS):
                direct_copy(g * PAIRS + j).wait_recv()

        @pl.when(s == 3)
        def _():
            for j in range(PAIRS):
                zero_copy(g * PAIRS + j).wait()

        return carry

    lax.fori_loop(0, HK, drain, 0)

    for i in range(len(SIDE)):
        pl.when(helps[i])(side_back(i).wait_send)


def hand_out(a, b, c, a_out, b_out, c_out, sem):
    copies = [
        pltpu.make_async_copy(b, b_out, sem.at[0]),
        pltpu.make_async_copy(c, c_out, sem.at[1]),
    ]
    for i in range(8):
        rows = pl.ds(i * (TOK // 8), TOK // 8)
        copies.append(pltpu.make_async_copy(a.at[0, rows], a_out.at[0, rows], sem.at[2 + i]))
    for copy in copies:
        copy.start()
    for copy in copies:
        copy.wait()


def solution(mesh):
    n_ctx = mesh.shape["ctx"]
    freq = np.broadcast_to(yarn_frequencies()[:, None], (HALF, TOK)).copy()

    def shards(q, k, v, o, do, doc_start, fetch_list):
        any_spec = pl.BlockSpec(memory_space=pl.ANY)
        hbm = pl.BlockSpec(memory_space=pltpu.HBM)
        vmem = pl.BlockSpec(memory_space=pltpu.VMEM)
        dma = pltpu.SemaphoreType.DMA
        results = pl.pallas_call(
            functools.partial(kernel, n_ctx),
            out_shape=(
                pltpu.VMEM((1, TOK, HQ * HD), BF16),
                pltpu.VMEM((1, TOK, HK * HD), BF16),
                pltpu.VMEM((1, TOK, HK * HD), BF16),
            ),
            in_specs=[hbm] * 8,
            out_specs=(vmem,) * 3,
            scratch_shapes=[
                pltpu.VMEM((1, TOK), jnp.int32),
                pltpu.VMEM((1, 2), jnp.int32),
                pltpu.VMEM((HALF, TOK), F32),
                pltpu.VMEM((HK, TOK, RATIO * HD), BF16),
                pltpu.VMEM((HK, TOK, RATIO * HD), BF16),
                pltpu.VMEM((HK, TOK, RATIO * HD), BF16),
                pltpu.VMEM((3, HK, 2, TOK, HD), BF16),
                pltpu.VMEM((HQ, TOK, HD), BF16),
                pltpu.VMEM((HQ, TOK, 2 * HD), BF16),
                pltpu.VMEM((3 * TOK, TOK), F32),
                pltpu.VMEM((2, HALF, TOK), F32),
                pltpu.VMEM((3, TOK, HD), F32),
                pltpu.VMEM((3, TOK, HD), F32),
                pltpu.VMEM((HD, 3 * TOK), BF16),
                pltpu.VMEM((3 * TOK, RATIO * TOK), BF16),
                pltpu.VMEM((3 * TOK, RATIO * TOK), BF16),
                pltpu.VMEM((HK, 2, TOK, HD), F32),
                pltpu.VMEM((2, HK, 2, TOK, HD), BF16),
                pltpu.VMEM((2, HK, 2, TOK, HD), BF16),
                pltpu.VMEM((HK * PAIRS, TOK, 2 * HD), BF16),
                pltpu.VMEM((2, HK, TOK, 2 * HD), BF16),
                pltpu.VMEM((len(SIDE), TOK, 2 * HD), BF16),
                pltpu.SemaphoreType.REGULAR,
                pltpu.SemaphoreType.REGULAR,
                dma((3,)),
                dma((2, HK)),
                dma((3, HK)),
                dma((2, HK, 2)),
                dma((2, HK, 2)),
                dma((2, HK)),
                dma((2, HK)),
                dma((HK * PAIRS,)),
                dma((HK * PAIRS,)),
                dma((2, HK)),
                dma((2, HK)),
                dma((len(SIDE),)),
                dma((len(SIDE),)),
            ],
            compiler_params=pltpu.CompilerParams(
                collective_id=0, has_side_effects=True, vmem_limit_bytes=28 << 20
            ),
            cost_estimate=pl.CostEstimate(flops=2_000_000_000, bytes_accessed=5_000_000, transcendentals=1_600_000),
        )(*(pltpu.with_memory_space_constraint(x, pltpu.HBM) for x in (doc_start.reshape(1, TOK), fetch_list, jnp.asarray(freq), q, k, v, o, do)))
        return pl.pallas_call(
            hand_out,
            out_shape=tuple(jax.ShapeDtypeStruct((1, TOK, n * HD), BF16) for n in (HQ, HK, HK)),
            in_specs=[vmem] * 3,
            out_specs=(hbm,) * 3,
            scratch_shapes=[dma((10,))],
            compiler_params=pltpu.CompilerParams(vmem_limit_bytes=1 << 20),
            cost_estimate=pl.CostEstimate(flops=0, bytes_accessed=2_600_000, transcendentals=0),
        )(*results)

    return jax.shard_map(
        shards,
        mesh=mesh,
        in_specs=(
            P("section", "ctx", None),
            P("section", "ctx", None),
            P("section", "ctx", None),
            P("section", "ctx", None),
            P("section", "ctx", None),
            P("ctx"),
            P("ctx", None),
        ),
        out_specs=(P("section", "ctx", None),) * 3,
        check_vma=False,
    )
```

```python
import functools
import math

import jax
import jax.numpy as jnp
import numpy as np
from jax import lax
from jax.experimental import pallas as pl
from jax.experimental.pallas import tpu as pltpu
from jax.sharding import PartitionSpec as P

HQ = 32
HK = 4
HD = 128
TOK = 128
RATIO = HQ // HK
PAIRS = RATIO // 2
HALF = HD // 2
ROPE_BASE = 1000000.0
TRAINED_CONTEXT = 32768.0
YARN_FACTOR = 4.0
NEG_LARGE = -1.0e30
SCALE = HD**-0.5
N_LONG = 3
CHAIN = 16
SIDE = (7, 10)
RELAY = 1
MESH = pl.DeviceIdType.MESH
F32 = jnp.float32
BF16 = jnp.bfloat16


def yarn_frequencies():
    def correction(rotations):
        return HD * math.log(TRAINED_CONTEXT / (rotations * 2.0 * math.pi)) / (2.0 * math.log(ROPE_BASE))

    lower = max(math.floor(correction(32.0)), 0)
    upper = min(math.ceil(correction(1.0)), HD - 1)
    spread = max(upper - lower, 0.001)
    index = np.arange(HALF, dtype=np.float64)
    base = ROPE_BASE ** (-2.0 * index / HD)
    ramp = np.clip((index - lower) / spread, 0.0, 1.0)
    return (base / YARN_FACTOR * ramp + base * (1.0 - ramp)).astype(np.float32)


def sin_cos(x):
    n = jnp.floor(x * (2.0 / math.pi) + 0.5)
    r = x - n * 1.5703125
    r = r - n * 4.83751296997070312e-4
    r = r - n * 7.54978995489188216e-8
    z = r * r
    sin = r + r * z * (-1.6666654611e-1 + z * (8.3321608736e-3 + z * -1.9515295891e-4))
    cos = 1.0 - 0.5 * z + z * z * (4.166664568298827e-2 + z * (-1.388731625493765e-3 + z * 2.443315711809948e-5))
    q = n.astype(jnp.int32) & 3
    odd = (q & 1) == 1
    s = jnp.where(odd, cos, sin)
    c = jnp.where(odd, sin, cos)
    return jnp.where(q >= 2, -s, s), jnp.where((q == 1) | (q == 2), -c, c)


def long_pair(i, early):
    return i * PAIRS + 1 - jnp.minimum(i, 1) - 2 * early * (i // 2)


def dot_t(a, b):
    return lax.dot_general(a, b, (((1,), (1,)), ((), ())), preferred_element_type=F32)


def dot(a, b):
    return jnp.dot(a, b, preferred_element_type=F32)


def kernel(
    n_ctx,
    doc_hbm, fetch_hbm, freq_hbm, q_hbm, k_hbm, v_hbm, o_hbm, do_hbm,
    out_ref, dk_ref, dv_ref,
    doc_ref, fetch_ref, freq_ref, q_in, o_in, do_in,
    kv, qr, doz, bias, tab_t, tab_c, tab_s, k_t, p_win, ds_win, own, back_out, back_in, dq, relay, side,
    ready, helped, small_sem, kv_sem, query_sem, kv_send, kv_recv, back_send, back_recv, dq_send, out_recv, relay_recv, relay_send, side_recv, side_send,
):
    c = lax.axis_index("ctx")
    s = lax.axis_index("section")

    place = lax.rem(c, CHAIN)
    first_chip = (place < 2) & (s >= 1)
    helps = [(place // 2 == i + 1) & (s <= 2) for i in range(len(SIDE))]

    small = [
        pltpu.make_async_copy(doc_hbm, doc_ref, small_sem.at[0]),
        pltpu.make_async_copy(freq_hbm, freq_ref, small_sem.at[1]),
        pltpu.make_async_copy(fetch_hbm, fetch_ref, small_sem.at[2]),
    ]

    def head_cols(ref, g):
        return ref.at[0, :, pl.ds(pl.multiple_of(g * HD, HD), HD)]

    def kv_loads(g):
        return [
            pltpu.make_async_copy(head_cols(x, g), kv.at[0, g, i], kv_sem.at[i, g]) for i, x in enumerate((k_hbm, v_hbm))
        ]

    def query_loads(g):
        cols = pl.ds(pl.multiple_of(g * RATIO * HD, RATIO * HD), RATIO * HD)
        return [
            pltpu.make_async_copy(x.at[0, :, cols], y.at[g], query_sem.at[i, g])
            for i, (x, y) in enumerate(((q_hbm, q_in), (do_hbm, do_in), (o_hbm, o_in)))
        ]

    for load in small:
        load.start()
    for g in range(HK):
        for load in kv_loads(g) + query_loads(g):
            load.start()

    barrier = pltpu.get_barrier_semaphore()
    for d in (1, 2):
        @pl.when(c >= d)
        def _():
            pl.semaphore_signal(barrier, inc=1, device_id=(c - d, s), device_id_type=MESH)
    for me, others in ((0, (1, 2, 3)), (1, (2,)), (2, (3,))):
        @pl.when(s == me)
        def _():
            for other in others:
                pl.semaphore_signal(barrier, inc=1, device_id=(c, other), device_id_type=MESH)

    @pl.when(first_chip)
    def _():
        for i in range(len(SIDE)):
            pl.semaphore_signal(barrier, inc=1, device_id=(c + 2 * i + 2, s - 1), device_id_type=MESH)

    greeted = s - s // 3 + sum(h.astype(jnp.int32) for h in helps) + (c < n_ctx - 1).astype(jnp.int32) + (c < n_ctx - 2).astype(jnp.int32)

    @pl.when(greeted > 0)
    def _():
        pl.semaphore_wait(barrier, greeted)

    for me, others in ((1, (0,)), (2, (0, 1))):
        @pl.when(s == me)
        def _():
            for other in others:
                pl.semaphore_signal(ready, inc=1, device_id=(c, other), device_id_type=MESH)

    for i in range(len(SIDE)):
        @pl.when(helps[i])
        def _():
            pl.semaphore_signal(helped, inc=1, device_id=(c - 2 * i - 2, s + 1), device_id_type=MESH)

    def kv_copies(g, d):
        return [
            pltpu.make_async_remote_copy(
                src_ref=head_cols(x, g), dst_ref=kv.at[d, g, i],
                send_sem=kv_send.at[d - 1, g, i], recv_sem=kv_recv.at[d - 1, g, i],
                device_id=(c + d, s), device_id_type=MESH,
            )
            for i, x in enumerate((k_hbm, v_hbm))
        ]

    for g in range(1):
        for d in (1, 2):
            @pl.when(c < n_ctx - d)
            def _():
                for copy in kv_copies(g, d):
                    copy.start()
    for d in (1, 2):
        @pl.when(c < d)
        def _():
            kv[d] = jnp.zeros((HK, 2, TOK, HD), BF16)
        @pl.when(c >= n_ctx - d)
        def _():
            back_in[d - 1] = jnp.zeros((HK, 2, TOK, HD), BF16)

    for load in small:
        load.wait()
    first = c * TOK
    lane = lax.broadcasted_iota(jnp.int32, (1, TOK), 1)
    lane_t = lane + first
    start = doc_ref[...]
    factor = 0.1 * math.log(YARN_FACTOR) + 1.0
    low = lax.broadcasted_iota(jnp.int32, (TOK, HD), 1) < HALF
    for d in range(3):
        position = lane_t - start if d == 0 else jnp.maximum(lane_t - d * TOK - start[:, 0:1], 0)
        sin, cos = sin_cos(position.astype(F32) * freq_ref[...])
        sin = sin * factor
        cos = cos * factor
        if d == 0:
            tab_t[0] = cos * SCALE
            tab_t[1] = sin * SCALE
        turned = jnp.concatenate([cos, sin], axis=0).T
        swapped = pltpu.roll(turned, HALF, 1)
        tab_c[d] = jnp.where(low, turned, swapped)
        tab_s[d] = jnp.where(low, -swapped, turned)

    def rope(x, d):
        x = x.astype(F32)
        return (x * tab_c[d] + pltpu.roll(x, HALF, 1) * tab_s[d]).astype(BF16)

    def zero_copy(p):
        return pltpu.make_async_copy(
            relay.at[0, 0], out_ref.at[0, :, pl.ds(pl.multiple_of(p * 2 * HD, 2 * HD), 2 * HD)], out_recv.at[p]
        )

    @pl.when(s == 3)
    def _():
        relay[0, 0] = jnp.zeros((TOK, 2 * HD), BF16)

        def put(p, carry):
            zero_copy(p).start()
            return carry

        lax.fori_loop(0, HK * PAIRS, put, 0)

    row = lax.broadcasted_iota(jnp.int32, (TOK, TOK), 0)
    for d in range(3):
        u = first - d * TOK + row
        allowed = (u >= start) & (u <= lane_t)
        if d > 0:
            allowed = allowed & (fetch_ref[:, d - 1 : d] == 1)
        bias[d * TOK : (d + 1) * TOK, :] = jnp.where(allowed, 0.0, NEG_LARGE)

    for g in range(HK):
        for load in query_loads(g) + kv_loads(g):
            load.wait()

    def prepare(g):
        for i in range(RATIO):
            h = g * RATIO + i
            cols = slice(i * HD, (i + 1) * HD)
            qr[h] = rope(q_in[g, :, cols], 0)
            grad = do_in[g, :, cols]
            prod = grad.astype(F32) * o_in[g, :, cols].astype(F32)
            prod = prod + pltpu.roll(prod, HALF, 1)
            high = prod.astype(BF16).astype(F32)
            doz[h, :, 0:HD] = grad
            doz[h, :, HD : 2 * HD] = jnp.where(low, high, prod - high).astype(BF16)

    lax.fori_loop(0, HK, lambda g, c: (prepare(g), c)[1], 0)

    for g in range(1, HK):
        for d in (1, 2):
            @pl.when(c < n_ctx - d)
            def _():
                for copy in kv_copies(g, d):
                    copy.start()

    def out_cols(p):
        return out_ref.at[0, :, pl.ds(pl.multiple_of(p * 2 * HD, 2 * HD), 2 * HD)]

    def direct_copy(p):
        return pltpu.make_async_remote_copy(
            src_ref=dq.at[p], dst_ref=out_cols(p), send_sem=dq_send.at[p], recv_sem=out_recv.at[p],
            device_id=(c, s - 1), device_id_type=MESH,
        )

    def long_copy(g):
        return pltpu.make_async_remote_copy(
            src_ref=dq.at[long_pair(g, s // 3)], dst_ref=relay.at[s // 3, g],
            send_sem=dq_send.at[long_pair(g, s // 3)], recv_sem=relay_recv.at[s // 3, g],
            device_id=(c, 2 * (1 - s // 2)), device_id_type=MESH,
        )

    def side_copy(i):
        return pltpu.make_async_remote_copy(
            src_ref=dq.at[SIDE[i]], dst_ref=side.at[i],
            send_sem=dq_send.at[SIDE[i]], recv_sem=side_recv.at[i],
            device_id=(c + 2 * i + 2, s - 1), device_id_type=MESH,
        )

    def side_back(i):
        return pltpu.make_async_remote_copy(
            src_ref=side.at[i], dst_ref=out_cols(SIDE[i]),
            send_sem=side_send.at[i], recv_sem=out_recv.at[SIDE[i]],
            device_id=(c - 2 * i - 2, s), device_id_type=MESH,
        )

    def relay_copy(slot, g, target):
        p = long_pair(g, slot)
        return pltpu.make_async_remote_copy(
            src_ref=relay.at[slot, g], dst_ref=out_cols(p),
            send_sem=relay_send.at[slot, g], recv_sem=out_recv.at[p],
            device_id=(c, target), device_id_type=MESH,
        )

    def arrival(slot, g):
        return pltpu.make_async_remote_copy(
            src_ref=dq.at[0], dst_ref=relay.at[slot, g],
            send_sem=dq_send.at[0], recv_sem=relay_recv.at[slot, g],
            device_id=(c, 0), device_id_type=MESH,
        )

    def forward(g):
        @pl.when(s == 0)
        def _():
            @pl.when(g == 0)
            def _():
                pl.semaphore_wait(ready, 2)

            arrival(0, g).wait_recv()
            relay_copy(0, g, 1).start()
            arrival(1, g).wait_recv()
            relay_copy(1, g, 2).start()

        @pl.when(s == 2)
        def _():
            arrival(0, g).wait_recv()
            relay_copy(0, g, 0).start()

    def back_copy(g, d):
        return pltpu.make_async_remote_copy(
            src_ref=back_out.at[d - 1, g], dst_ref=back_in.at[d - 1, g],
            send_sem=back_send.at[d - 1, g], recv_sem=back_recv.at[d - 1, g],
            device_id=(c - d, s), device_id_type=MESH,
        )

    def group(g, carry):
        for d in (1, 2):
            @pl.when(c >= d)
            def _():
                for copy in kv_copies(g, d):
                    copy.wait_recv()

        k_win = jnp.concatenate([rope(kv[d, g, 0], d) for d in range(3)], axis=0)
        v_win = jnp.concatenate([kv[d, g, 1] for d in range(3)], axis=0)
        v_one = jnp.concatenate([v_win, jnp.full((3 * TOK, HD), -1.0, BF16)], axis=1)
        k_t[...] = k_win.T
        b = bias[...]
        b = jnp.concatenate([b, b], axis=1)

        def products(j):
            h = g * RATIO + 2 * j
            qp = qr[pl.ds(h, 2)].reshape(2 * TOK, HD)
            dp_in = doz[pl.ds(h, 2)].reshape(2 * TOK, 2 * HD)
            return dot_t(k_win, qp), dot_t(v_one, dp_in)

        ahead = products(0)
        for j in range(PAIRS):
            p = g * PAIRS + j
            sc, dp = ahead
            if j + 1 < PAIRS:
                ahead = products(j + 1)
            sc = sc * (SCALE * math.log2(math.e)) + b
            e = jnp.exp2(sc - jnp.max(sc, axis=0, keepdims=True))
            prob = e * (1.0 / jnp.sum(e, axis=0, keepdims=True))
            ds = (prob * dp).astype(BF16)
            p_win[:, 2 * j * TOK : 2 * (j + 1) * TOK] = prob.astype(BF16)
            ds_win[:, 2 * j * TOK : 2 * (j + 1) * TOK] = ds
            if j == 0:
                @pl.when(first_chip & (g == 1))
                def _():
                    pl.semaphore_wait(helped, len(SIDE))

            if j == 1:
                @pl.when((s == 1) & (g == 0))
                def _():
                    pl.semaphore_wait(ready, 1)

            @pl.when(s >= 1)
            def _():
                turned_grad = dot(k_t[...], ds_win[:, 2 * j * TOK : 2 * (j + 1) * TOK])
                for i in range(2):
                    x = turned_grad[:HALF, i * TOK : (i + 1) * TOK]
                    y = turned_grad[HALF:, i * TOK : (i + 1) * TOK]
                    grad = jnp.concatenate(
                        [x * tab_t[0] + y * tab_t[1], y * tab_t[0] - x * tab_t[1]], axis=0
                    )
                    dq[p, :, i * HD : (i + 1) * HD] = grad.T.astype(BF16)
                if j == 0:
                    far = (g == 1) | ((g == 2) & (s < 3))
                    pl.when(far)(long_copy(g).start)
                    pl.when(jnp.logical_not(far))(direct_copy(p).start)
                elif j == 1:
                    pl.when(g == 0)(long_copy(g).start)
                    pl.when(g >= 1)(direct_copy(p).start)
                elif j == 2:
                    far = (g == 1) & (s == 3)
                    aside = (g == 2) & first_chip
                    pl.when(far)(long_copy(2).start)
                    pl.when(aside)(side_copy(1).start)
                    pl.when((g < 3) & jnp.logical_not(far | aside))(direct_copy(p).start)
                else:
                    aside = (g == 1) & first_chip
                    pl.when(aside)(side_copy(0).start)
                    pl.when((g < 2) & jnp.logical_not(aside))(direct_copy(p).start)

        dk = dot(ds_win[...], qr[pl.ds(g * RATIO, RATIO)].reshape(RATIO * TOK, HD))
        dv = dot(p_win[...], doz[pl.ds(g * RATIO, RATIO), :, 0:HD].reshape(RATIO * TOK, HD))
        own[g, 0] = dk[:TOK]
        own[g, 1] = dv[:TOK]
        for d in (1, 2):
            back_out[d - 1, g, 0] = dk[d * TOK : (d + 1) * TOK].astype(BF16)
            back_out[d - 1, g, 1] = dv[d * TOK : (d + 1) * TOK].astype(BF16)
            pl.when(c >= d)(back_copy(g, d).start)

        pl.when((s == 2) & (g >= 1))(lambda: forward(g - 1))
        due = g - 2

        @pl.when((s == 0) & (due >= 0))
        def _():
            forward(due)

        return carry

    lax.fori_loop(0, HK, group, 0)

    pl.when(s == 0)(lambda: forward(N_LONG - 1))


    for i, rest in enumerate(((11,), (14, 15))):
        @pl.when(helps[i])
        def _():
            side_copy(i).wait_recv()
            side_back(i).start()

        @pl.when(s >= 1)
        def _():
            for p in rest:
                direct_copy(p).start()


    def finish(g, carry):
        for d in (1, 2):
            pl.when(c < n_ctx - d)(back_copy(g, d).wait_recv)
        dk = own[g, 0] + back_in[0, g, 0].astype(F32) + back_in[1, g, 0].astype(F32)
        dv = own[g, 1] + back_in[0, g, 1].astype(F32) + back_in[1, g, 1].astype(F32)
        dk = dk * SCALE
        cols = pl.ds(pl.multiple_of(g * HD, HD), HD)
        dk_ref[0, :, cols] = (dk * tab_c[0] - pltpu.roll(dk, HALF, 1) * tab_s[0]).astype(BF16)
        dv_ref[0, :, cols] = dv.astype(BF16)
        return carry

    lax.fori_loop(0, HK, finish, 0)

    def drain(g, carry):
        for d in (1, 2):
            @pl.when(c < n_ctx - d)
            def _():
                for copy in kv_copies(g, d):
                    copy.wait_send()

            pl.when(c >= d)(back_copy(g, d).wait_send)

        @pl.when(s >= 1)
        def _():
            for j in range(PAIRS):
                direct_copy(g * PAIRS + j).wait_send()

        @pl.when((s == 0) & (g < N_LONG))
        def _():
            relay_copy(0, g, 1).wait_send()
            relay_copy(1, g, 2).wait_send()

        @pl.when((s == 2) & (g < N_LONG))
        def _():
            relay_copy(0, g, 0).wait_send()

        @pl.when(s <= 2)
        def _():
            for j in range(PAIRS):
                direct_copy(g * PAIRS + j).wait_recv()

        @pl.when(s == 3)
        def _():
            for j in range(PAIRS):
                zero_copy(g * PAIRS + j).wait()

        return carry

    lax.fori_loop(0, HK, drain, 0)

    for i in range(len(SIDE)):
        pl.when(helps[i])(side_back(i).wait_send)


def hand_out(a, b, c, a_out, b_out, c_out, sem):
    copies = [
        pltpu.make_async_copy(b, b_out, sem.at[0]),
        pltpu.make_async_copy(c, c_out, sem.at[1]),
    ]
    for i in range(8):
        rows = pl.ds(i * (TOK // 8), TOK // 8)
        copies.append(pltpu.make_async_copy(a.at[0, rows], a_out.at[0, rows], sem.at[2 + i]))
    for copy in copies:
        copy.start()
    for copy in copies:
        copy.wait()


def solution(mesh):
    n_ctx = mesh.shape["ctx"]
    freq = np.broadcast_to(yarn_frequencies()[:, None], (HALF, TOK)).copy()

    def shards(q, k, v, o, do, doc_start, fetch_list):
        any_spec = pl.BlockSpec(memory_space=pl.ANY)
        hbm = pl.BlockSpec(memory_space=pltpu.HBM)
        vmem = pl.BlockSpec(memory_space=pltpu.VMEM)
        dma = pltpu.SemaphoreType.DMA
        results = pl.pallas_call(
            functools.partial(kernel, n_ctx),
            out_shape=(
                pltpu.VMEM((1, TOK, HQ * HD), BF16),
                pltpu.VMEM((1, TOK, HK * HD), BF16),
                pltpu.VMEM((1, TOK, HK * HD), BF16),
            ),
            in_specs=[hbm] * 8,
            out_specs=(vmem,) * 3,
            scratch_shapes=[
                pltpu.VMEM((1, TOK), jnp.int32),
                pltpu.VMEM((1, 2), jnp.int32),
                pltpu.VMEM((HALF, TOK), F32),
                pltpu.VMEM((HK, TOK, RATIO * HD), BF16),
                pltpu.VMEM((HK, TOK, RATIO * HD), BF16),
                pltpu.VMEM((HK, TOK, RATIO * HD), BF16),
                pltpu.VMEM((3, HK, 2, TOK, HD), BF16),
                pltpu.VMEM((HQ, TOK, HD), BF16),
                pltpu.VMEM((HQ, TOK, 2 * HD), BF16),
                pltpu.VMEM((3 * TOK, TOK), F32),
                pltpu.VMEM((2, HALF, TOK), F32),
                pltpu.VMEM((3, TOK, HD), F32),
                pltpu.VMEM((3, TOK, HD), F32),
                pltpu.VMEM((HD, 3 * TOK), BF16),
                pltpu.VMEM((3 * TOK, RATIO * TOK), BF16),
                pltpu.VMEM((3 * TOK, RATIO * TOK), BF16),
                pltpu.VMEM((HK, 2, TOK, HD), F32),
                pltpu.VMEM((2, HK, 2, TOK, HD), BF16),
                pltpu.VMEM((2, HK, 2, TOK, HD), BF16),
                pltpu.VMEM((HK * PAIRS, TOK, 2 * HD), BF16),
                pltpu.VMEM((2, HK, TOK, 2 * HD), BF16),
                pltpu.VMEM((len(SIDE), TOK, 2 * HD), BF16),
                pltpu.SemaphoreType.REGULAR,
                pltpu.SemaphoreType.REGULAR,
                dma((3,)),
                dma((2, HK)),
                dma((3, HK)),
                dma((2, HK, 2)),
                dma((2, HK, 2)),
                dma((2, HK)),
                dma((2, HK)),
                dma((HK * PAIRS,)),
                dma((HK * PAIRS,)),
                dma((2, HK)),
                dma((2, HK)),
                dma((len(SIDE),)),
                dma((len(SIDE),)),
            ],
            compiler_params=pltpu.CompilerParams(
                collective_id=0, has_side_effects=True, vmem_limit_bytes=28 << 20
            ),
            cost_estimate=pl.CostEstimate(flops=2_000_000_000, bytes_accessed=5_000_000, transcendentals=1_600_000),
        )(*(pltpu.with_memory_space_constraint(x, pltpu.HBM) for x in (doc_start.reshape(1, TOK), fetch_list, jnp.asarray(freq), q, k, v, o, do)))
        return pl.pallas_call(
            hand_out,
            out_shape=tuple(jax.ShapeDtypeStruct((1, TOK, n * HD), BF16) for n in (HQ, HK, HK)),
            in_specs=[vmem] * 3,
            out_specs=(hbm,) * 3,
            scratch_shapes=[dma((10,))],
            compiler_params=pltpu.CompilerParams(vmem_limit_bytes=1 << 20),
            cost_estimate=pl.CostEstimate(flops=0, bytes_accessed=2_600_000, transcendentals=0),
        )(*results)

    return jax.shard_map(
        shards,
        mesh=mesh,
        in_specs=(
            P("section", "ctx", None),
            P("section", "ctx", None),
            P("section", "ctx", None),
            P("section", "ctx", None),
            P("section", "ctx", None),
            P("ctx"),
            P("ctx", None),
        ),
        out_specs=(P("section", "ctx", None),) * 3,
        check_vma=False,
    )
```

```python
import functools
import math

import jax
import jax.numpy as jnp
import numpy as np
from jax import lax
from jax.experimental import pallas as pl
from jax.experimental.pallas import tpu as pltpu
from jax.sharding import PartitionSpec as P

HQ = 32
HK = 4
HD = 128
TOK = 128
RATIO = HQ // HK
PAIRS = RATIO // 2
HALF = HD // 2
ROPE_BASE = 1000000.0
TRAINED_CONTEXT = 32768.0
YARN_FACTOR = 4.0
NEG_LARGE = -1.0e30
SCALE = HD**-0.5
N_LONG = 3
CHAIN = 16
SIDE = (7, 10)
RELAY = 1
MESH = pl.DeviceIdType.MESH
F32 = jnp.float32
BF16 = jnp.bfloat16


def yarn_frequencies():
    def correction(rotations):
        return HD * math.log(TRAINED_CONTEXT / (rotations * 2.0 * math.pi)) / (2.0 * math.log(ROPE_BASE))

    lower = max(math.floor(correction(32.0)), 0)
    upper = min(math.ceil(correction(1.0)), HD - 1)
    spread = max(upper - lower, 0.001)
    index = np.arange(HALF, dtype=np.float64)
    base = ROPE_BASE ** (-2.0 * index / HD)
    ramp = np.clip((index - lower) / spread, 0.0, 1.0)
    return (base / YARN_FACTOR * ramp + base * (1.0 - ramp)).astype(np.float32)


def sin_cos(x):
    n = jnp.floor(x * (2.0 / math.pi) + 0.5)
    r = x - n * 1.5703125
    r = r - n * 4.83751296997070312e-4
    r = r - n * 7.54978995489188216e-8
    z = r * r
    sin = r + r * z * (-1.6666654611e-1 + z * (8.3321608736e-3 + z * -1.9515295891e-4))
    cos = 1.0 - 0.5 * z + z * z * (4.166664568298827e-2 + z * (-1.388731625493765e-3 + z * 2.443315711809948e-5))
    q = n.astype(jnp.int32) & 3
    odd = (q & 1) == 1
    s = jnp.where(odd, cos, sin)
    c = jnp.where(odd, sin, cos)
    return jnp.where(q >= 2, -s, s), jnp.where((q == 1) | (q == 2), -c, c)


def long_pair(i, early):
    return i * PAIRS + 1 - jnp.minimum(i, 1) - 2 * early * (i // 2)


def dot_t(a, b):
    return lax.dot_general(a, b, (((1,), (1,)), ((), ())), preferred_element_type=F32)


def dot(a, b):
    return jnp.dot(a, b, preferred_element_type=F32)


def kernel(
    n_ctx,
    doc_hbm, fetch_hbm, freq_hbm, q_hbm, k_hbm, v_hbm, o_hbm, do_hbm,
    out_ref, dk_ref, dv_ref,
    doc_ref, fetch_ref, freq_ref, q_in, o_in, do_in,
    kv, qr, doz, bias, tab_t, tab_c, tab_s, k_t, p_win, ds_win, own, back_out, back_in, dq, relay, side,
    ready, helped, small_sem, kv_sem, query_sem, kv_send, kv_recv, back_send, back_recv, dq_send, out_recv, relay_recv, relay_send, side_recv, side_send,
):
    c = lax.axis_index("ctx")
    s = lax.axis_index("section")

    place = lax.rem(c, CHAIN)
    first_chip = (place < 2) & (s >= 1)
    helps = [(place // 2 == i + 1) & (s <= 2) for i in range(len(SIDE))]

    small = [
        pltpu.make_async_copy(doc_hbm, doc_ref, small_sem.at[0]),
        pltpu.make_async_copy(freq_hbm, freq_ref, small_sem.at[1]),
        pltpu.make_async_copy(fetch_hbm, fetch_ref, small_sem.at[2]),
    ]

    def head_cols(ref, g):
        return ref.at[0, :, pl.ds(pl.multiple_of(g * HD, HD), HD)]

    def kv_loads(g):
        return [
            pltpu.make_async_copy(head_cols(x, g), kv.at[0, g, i], kv_sem.at[i, g]) for i, x in enumerate((k_hbm, v_hbm))
        ]

    def query_loads(g):
        cols = pl.ds(pl.multiple_of(g * RATIO * HD, RATIO * HD), RATIO * HD)
        return [
            pltpu.make_async_copy(x.at[0, :, cols], y.at[g], query_sem.at[i, g])
            for i, (x, y) in enumerate(((q_hbm, q_in), (do_hbm, do_in), (o_hbm, o_in)))
        ]

    for load in small:
        load.start()
    for g in range(HK):
        for load in kv_loads(g) + query_loads(g):
            load.start()

    barrier = pltpu.get_barrier_semaphore()
    for d in (1, 2):
        @pl.when(c >= d)
        def _():
            pl.semaphore_signal(barrier, inc=1, device_id=(c - d, s), device_id_type=MESH)
    for me, others in ((0, (1, 2, 3)), (1, (2,)), (2, (3,))):
        @pl.when(s == me)
        def _():
            for other in others:
                pl.semaphore_signal(barrier, inc=1, device_id=(c, other), device_id_type=MESH)

    @pl.when(first_chip)
    def _():
        for i in range(len(SIDE)):
            pl.semaphore_signal(barrier, inc=1, device_id=(c + 2 * i + 2, s - 1), device_id_type=MESH)

    greeted = s - s // 3 + sum(h.astype(jnp.int32) for h in helps) + (c < n_ctx - 1).astype(jnp.int32) + (c < n_ctx - 2).astype(jnp.int32)

    @pl.when(greeted > 0)
    def _():
        pl.semaphore_wait(barrier, greeted)

    for me, others in ((1, (0,)), (2, (0, 1))):
        @pl.when(s == me)
        def _():
            for other in others:
                pl.semaphore_signal(ready, inc=1, device_id=(c, other), device_id_type=MESH)

    for i in range(len(SIDE)):
        @pl.when(helps[i])
        def _():
            pl.semaphore_signal(helped, inc=1, device_id=(c - 2 * i - 2, s + 1), device_id_type=MESH)

    def kv_copies(g, d):
        return [
            pltpu.make_async_remote_copy(
                src_ref=head_cols(x, g), dst_ref=kv.at[d, g, i],
                send_sem=kv_send.at[d - 1, g, i], recv_sem=kv_recv.at[d - 1, g, i],
                device_id=(c + d, s), device_id_type=MESH,
            )
            for i, x in enumerate((k_hbm, v_hbm))
        ]

    for g in range(1):
        for d in (1, 2):
            @pl.when(c < n_ctx - d)
            def _():
                for copy in kv_copies(g, d):
                    copy.start()
    for d in (1, 2):
        @pl.when(c < d)
        def _():
            kv[d] = jnp.zeros((HK, 2, TOK, HD), BF16)
        @pl.when(c >= n_ctx - d)
        def _():
            back_in[d - 1] = jnp.zeros((HK, 2, TOK, HD), BF16)

    for load in small:
        load.wait()
    first = c * TOK
    lane = lax.broadcasted_iota(jnp.int32, (1, TOK), 1)
    lane_t = lane + first
    start = doc_ref[...]
    factor = 0.1 * math.log(YARN_FACTOR) + 1.0
    low = lax.broadcasted_iota(jnp.int32, (TOK, HD), 1) < HALF
    for d in range(3):
        position = lane_t - start if d == 0 else jnp.maximum(lane_t - d * TOK - start[:, 0:1], 0)
        sin, cos = sin_cos(position.astype(F32) * freq_ref[...])
        sin = sin * factor
        cos = cos * factor
        if d == 0:
            tab_t[0] = cos * SCALE
            tab_t[1] = sin * SCALE
        turned = jnp.concatenate([cos, sin], axis=0).T
        swapped = pltpu.roll(turned, HALF, 1)
        tab_c[d] = jnp.where(low, turned, swapped)
        tab_s[d] = jnp.where(low, -swapped, turned)

    def rope(x, d):
        x = x.astype(F32)
        return (x * tab_c[d] + pltpu.roll(x, HALF, 1) * tab_s[d]).astype(BF16)

    def zero_copy(p):
        return pltpu.make_async_copy(
            relay.at[0, 0], out_ref.at[0, :, pl.ds(pl.multiple_of(p * 2 * HD, 2 * HD), 2 * HD)], out_recv.at[p]
        )

    @pl.when(s == 3)
    def _():
        relay[0, 0] = jnp.zeros((TOK, 2 * HD), BF16)

        def put(p, carry):
            zero_copy(p).start()
            return carry

        lax.fori_loop(0, HK * PAIRS, put, 0)

    row = lax.broadcasted_iota(jnp.int32, (TOK, TOK), 0)
    for d in range(3):
        u = first - d * TOK + row
        allowed = (u >= start) & (u <= lane_t)
        if d > 0:
            allowed = allowed & (fetch_ref[:, d - 1 : d] == 1)
        bias[d * TOK : (d + 1) * TOK, :] = jnp.where(allowed, 0.0, NEG_LARGE)

    for g in range(HK):
        for load in query_loads(g) + kv_loads(g):
            load.wait()

    def prepare(g):
        for i in range(RATIO):
            h = g * RATIO + i
            cols = slice(i * HD, (i + 1) * HD)
            qr[h] = rope(q_in[g, :, cols], 0)
            grad = do_in[g, :, cols]
            prod = grad.astype(F32) * o_in[g, :, cols].astype(F32)
            prod = prod + pltpu.roll(prod, HALF, 1)
            high = prod.astype(BF16).astype(F32)
            doz[h, :, 0:HD] = grad
            doz[h, :, HD : 2 * HD] = jnp.where(low, high, prod - high).astype(BF16)

    lax.fori_loop(0, HK, lambda g, c: (prepare(g), c)[1], 0)

    for g in range(1, HK):
        for d in (1, 2):
            @pl.when(c < n_ctx - d)
            def _():
                for copy in kv_copies(g, d):
                    copy.start()

    def out_cols(p):
        return out_ref.at[0, :, pl.ds(pl.multiple_of(p * 2 * HD, 2 * HD), 2 * HD)]

    def direct_copy(p):
        return pltpu.make_async_remote_copy(
            src_ref=dq.at[p], dst_ref=out_cols(p), send_sem=dq_send.at[p], recv_sem=out_recv.at[p],
            device_id=(c, s - 1), device_id_type=MESH,
        )

    def long_copy(g):
        return pltpu.make_async_remote_copy(
            src_ref=dq.at[long_pair(g, s // 3)], dst_ref=relay.at[s // 3, g],
            send_sem=dq_send.at[long_pair(g, s // 3)], recv_sem=relay_recv.at[s // 3, g],
            device_id=(c, 2 * (1 - s // 2)), device_id_type=MESH,
        )

    def side_copy(i):
        return pltpu.make_async_remote_copy(
            src_ref=dq.at[SIDE[i]], dst_ref=side.at[i],
            send_sem=dq_send.at[SIDE[i]], recv_sem=side_recv.at[i],
            device_id=(c + 2 * i + 2, s - 1), device_id_type=MESH,
        )

    def side_back(i):
        return pltpu.make_async_remote_copy(
            src_ref=side.at[i], dst_ref=out_cols(SIDE[i]),
            send_sem=side_send.at[i], recv_sem=out_recv.at[SIDE[i]],
            device_id=(c - 2 * i - 2, s), device_id_type=MESH,
        )

    def relay_copy(slot, g, target):
        p = long_pair(g, slot)
        return pltpu.make_async_remote_copy(
            src_ref=relay.at[slot, g], dst_ref=out_cols(p),
            send_sem=relay_send.at[slot, g], recv_sem=out_recv.at[p],
            device_id=(c, target), device_id_type=MESH,
        )

    def arrival(slot, g):
        return pltpu.make_async_remote_copy(
            src_ref=dq.at[0], dst_ref=relay.at[slot, g],
            send_sem=dq_send.at[0], recv_sem=relay_recv.at[slot, g],
            device_id=(c, 0), device_id_type=MESH,
        )

    def forward(g):
        @pl.when(s == 0)
        def _():
            @pl.when(g == 0)
            def _():
                pl.semaphore_wait(ready, 2)

            arrival(0, g).wait_recv()
            relay_copy(0, g, 1).start()
            arrival(1, g).wait_recv()
            relay_copy(1, g, 2).start()

        @pl.when(s == 2)
        def _():
            arrival(0, g).wait_recv()
            relay_copy(0, g, 0).start()

    def back_copy(g, d):
        return pltpu.make_async_remote_copy(
            src_ref=back_out.at[d - 1, g], dst_ref=back_in.at[d - 1, g],
            send_sem=back_send.at[d - 1, g], recv_sem=back_recv.at[d - 1, g],
            device_id=(c - d, s), device_id_type=MESH,
        )

    def group(g, carry):
        for d in (1, 2):
            @pl.when(c >= d)
            def _():
                for copy in kv_copies(g, d):
                    copy.wait_recv()

        k_win = jnp.concatenate([rope(kv[d, g, 0], d) for d in range(3)], axis=0)
        v_win = jnp.concatenate([kv[d, g, 1] for d in range(3)], axis=0)
        v_one = jnp.concatenate([v_win, jnp.full((3 * TOK, HD), -1.0, BF16)], axis=1)
        k_t[...] = k_win.T
        b = bias[...]
        b = jnp.concatenate([b, b], axis=1)

        def products(j):
            h = g * RATIO + 2 * j
            qp = qr[pl.ds(h, 2)].reshape(2 * TOK, HD)
            dp_in = doz[pl.ds(h, 2)].reshape(2 * TOK, 2 * HD)
            return dot_t(k_win, qp), dot_t(v_one, dp_in)

        ahead = products(0)
        for j in range(PAIRS):
            p = g * PAIRS + j
            sc, dp = ahead
            if j + 1 < PAIRS:
                ahead = products(j + 1)
            sc = sc * (SCALE * math.log2(math.e)) + b
            e = jnp.exp2(sc - jnp.max(sc, axis=0, keepdims=True))
            prob = e * (1.0 / jnp.sum(e, axis=0, keepdims=True))
            ds = (prob * dp).astype(BF16)
            p_win[:, 2 * j * TOK : 2 * (j + 1) * TOK] = prob.astype(BF16)
            ds_win[:, 2 * j * TOK : 2 * (j + 1) * TOK] = ds
            if j == 0:
                @pl.when(first_chip & (g == 1))
                def _():
                    pl.semaphore_wait(helped, len(SIDE))

            if j == 1:
                @pl.when((s == 1) & (g == 0))
                def _():
                    pl.semaphore_wait(ready, 1)

            @pl.when(s >= 1)
            def _():
                turned_grad = dot(k_t[...], ds_win[:, 2 * j * TOK : 2 * (j + 1) * TOK])
                for i in range(2):
                    x = turned_grad[:HALF, i * TOK : (i + 1) * TOK]
                    y = turned_grad[HALF:, i * TOK : (i + 1) * TOK]
                    grad = jnp.concatenate(
                        [x * tab_t[0] + y * tab_t[1], y * tab_t[0] - x * tab_t[1]], axis=0
                    )
                    dq[p, :, i * HD : (i + 1) * HD] = grad.T.astype(BF16)
                if j == 0:
                    far = (g == 1) | ((g == 2) & (s < 3))
                    pl.when(far)(long_copy(g).start)
                    pl.when(jnp.logical_not(far))(direct_copy(p).start)
                elif j == 1:
                    pl.when(g == 0)(long_copy(g).start)
                    pl.when(g >= 1)(direct_copy(p).start)
                elif j == 2:
                    far = (g == 1) & (s == 3)
                    aside = (g == 2) & first_chip
                    pl.when(far)(long_copy(2).start)
                    pl.when(aside)(side_copy(1).start)
                    pl.when(((g < 3) | first_chip) & jnp.logical_not(far | aside))(direct_copy(p).start)
                else:
                    aside = (g == 1) & first_chip
                    pl.when(aside)(side_copy(0).start)
                    pl.when(((g < 2) | first_chip) & jnp.logical_not(aside))(direct_copy(p).start)

        dk = dot(ds_win[...], qr[pl.ds(g * RATIO, RATIO)].reshape(RATIO * TOK, HD))
        dv = dot(p_win[...], doz[pl.ds(g * RATIO, RATIO), :, 0:HD].reshape(RATIO * TOK, HD))
        own[g, 0] = dk[:TOK]
        own[g, 1] = dv[:TOK]
        for d in (1, 2):
            back_out[d - 1, g, 0] = dk[d * TOK : (d + 1) * TOK].astype(BF16)
            back_out[d - 1, g, 1] = dv[d * TOK : (d + 1) * TOK].astype(BF16)
            pl.when(c >= d)(back_copy(g, d).start)

        pl.when((s == 2) & (g >= 1))(lambda: forward(g - 1))
        due = g - 2

        @pl.when((s == 0) & (due >= 0))
        def _():
            forward(due)

        return carry

    lax.fori_loop(0, HK, group, 0)

    pl.when(s == 0)(lambda: forward(N_LONG - 1))


    for i, rest in enumerate(((11,), (14, 15))):
        @pl.when(helps[i])
        def _():
            side_copy(i).wait_recv()
            side_back(i).start()

        @pl.when((s >= 1) & jnp.logical_not(first_chip))
        def _():
            for p in rest:
                direct_copy(p).start()


    def finish(g, carry):
        for d in (1, 2):
            pl.when(c < n_ctx - d)(back_copy(g, d).wait_recv)
        dk = own[g, 0] + back_in[0, g, 0].astype(F32) + back_in[1, g, 0].astype(F32)
        dv = own[g, 1] + back_in[0, g, 1].astype(F32) + back_in[1, g, 1].astype(F32)
        dk = dk * SCALE
        cols = pl.ds(pl.multiple_of(g * HD, HD), HD)
        dk_ref[0, :, cols] = (dk * tab_c[0] - pltpu.roll(dk, HALF, 1) * tab_s[0]).astype(BF16)
        dv_ref[0, :, cols] = dv.astype(BF16)
        return carry

    lax.fori_loop(0, HK, finish, 0)

    def drain(g, carry):
        for d in (1, 2):
            @pl.when(c < n_ctx - d)
            def _():
                for copy in kv_copies(g, d):
                    copy.wait_send()

            pl.when(c >= d)(back_copy(g, d).wait_send)

        @pl.when(s >= 1)
        def _():
            for j in range(PAIRS):
                direct_copy(g * PAIRS + j).wait_send()

        @pl.when((s == 0) & (g < N_LONG))
        def _():
            relay_copy(0, g, 1).wait_send()
            relay_copy(1, g, 2).wait_send()

        @pl.when((s == 2) & (g < N_LONG))
        def _():
            relay_copy(0, g, 0).wait_send()

        @pl.when(s <= 2)
        def _():
            for j in range(PAIRS):
                direct_copy(g * PAIRS + j).wait_recv()

        @pl.when(s == 3)
        def _():
            for j in range(PAIRS):
                zero_copy(g * PAIRS + j).wait()

        return carry

    lax.fori_loop(0, HK, drain, 0)

    for i in range(len(SIDE)):
        pl.when(helps[i])(side_back(i).wait_send)


def hand_out(a, b, c, a_out, b_out, c_out, sem):
    copies = [
        pltpu.make_async_copy(b, b_out, sem.at[0]),
        pltpu.make_async_copy(c, c_out, sem.at[1]),
    ]
    copies.append(pltpu.make_async_copy(a, a_out, sem.at[2]))
    for copy in copies:
        copy.start()
    for copy in copies:
        copy.wait()


def solution(mesh):
    n_ctx = mesh.shape["ctx"]
    freq = np.broadcast_to(yarn_frequencies()[:, None], (HALF, TOK)).copy()

    def shards(q, k, v, o, do, doc_start, fetch_list):
        any_spec = pl.BlockSpec(memory_space=pl.ANY)
        hbm = pl.BlockSpec(memory_space=pltpu.HBM)
        vmem = pl.BlockSpec(memory_space=pltpu.VMEM)
        dma = pltpu.SemaphoreType.DMA
        results = pl.pallas_call(
            functools.partial(kernel, n_ctx),
            out_shape=(
                pltpu.VMEM((1, TOK, HQ * HD), BF16),
                pltpu.VMEM((1, TOK, HK * HD), BF16),
                pltpu.VMEM((1, TOK, HK * HD), BF16),
            ),
            in_specs=[hbm] * 8,
            out_specs=(vmem,) * 3,
            scratch_shapes=[
                pltpu.VMEM((1, TOK), jnp.int32),
                pltpu.VMEM((1, 2), jnp.int32),
                pltpu.VMEM((HALF, TOK), F32),
                pltpu.VMEM((HK, TOK, RATIO * HD), BF16),
                pltpu.VMEM((HK, TOK, RATIO * HD), BF16),
                pltpu.VMEM((HK, TOK, RATIO * HD), BF16),
                pltpu.VMEM((3, HK, 2, TOK, HD), BF16),
                pltpu.VMEM((HQ, TOK, HD), BF16),
                pltpu.VMEM((HQ, TOK, 2 * HD), BF16),
                pltpu.VMEM((3 * TOK, TOK), F32),
                pltpu.VMEM((2, HALF, TOK), F32),
                pltpu.VMEM((3, TOK, HD), F32),
                pltpu.VMEM((3, TOK, HD), F32),
                pltpu.VMEM((HD, 3 * TOK), BF16),
                pltpu.VMEM((3 * TOK, RATIO * TOK), BF16),
                pltpu.VMEM((3 * TOK, RATIO * TOK), BF16),
                pltpu.VMEM((HK, 2, TOK, HD), F32),
                pltpu.VMEM((2, HK, 2, TOK, HD), BF16),
                pltpu.VMEM((2, HK, 2, TOK, HD), BF16),
                pltpu.VMEM((HK * PAIRS, TOK, 2 * HD), BF16),
                pltpu.VMEM((2, HK, TOK, 2 * HD), BF16),
                pltpu.VMEM((len(SIDE), TOK, 2 * HD), BF16),
                pltpu.SemaphoreType.REGULAR,
                pltpu.SemaphoreType.REGULAR,
                dma((3,)),
                dma((2, HK)),
                dma((3, HK)),
                dma((2, HK, 2)),
                dma((2, HK, 2)),
                dma((2, HK)),
                dma((2, HK)),
                dma((HK * PAIRS,)),
                dma((HK * PAIRS,)),
                dma((2, HK)),
                dma((2, HK)),
                dma((len(SIDE),)),
                dma((len(SIDE),)),
            ],
            compiler_params=pltpu.CompilerParams(
                collective_id=0, has_side_effects=True, vmem_limit_bytes=28 << 20
            ),
            cost_estimate=pl.CostEstimate(flops=2_000_000_000, bytes_accessed=5_000_000, transcendentals=1_600_000),
        )(*(pltpu.with_memory_space_constraint(x, pltpu.HBM) for x in (doc_start.reshape(1, TOK), fetch_list, jnp.asarray(freq), q, k, v, o, do)))
        return pl.pallas_call(
            hand_out,
            out_shape=tuple(jax.ShapeDtypeStruct((1, TOK, n * HD), BF16) for n in (HQ, HK, HK)),
            in_specs=[vmem] * 3,
            out_specs=(hbm,) * 3,
            scratch_shapes=[dma((3,))],
            compiler_params=pltpu.CompilerParams(vmem_limit_bytes=1 << 20),
            cost_estimate=pl.CostEstimate(flops=0, bytes_accessed=2_600_000, transcendentals=0),
        )(*results)

    return jax.shard_map(
        shards,
        mesh=mesh,
        in_specs=(
            P("section", "ctx", None),
            P("section", "ctx", None),
            P("section", "ctx", None),
            P("section", "ctx", None),
            P("section", "ctx", None),
            P("ctx"),
            P("ctx", None),
        ),
        out_specs=(P("section", "ctx", None),) * 3,
        check_vma=False,
    )
```

```python
import functools
import math

import jax
import jax.numpy as jnp
import numpy as np
from jax import lax
from jax.experimental import pallas as pl
from jax.experimental.pallas import tpu as pltpu
from jax.sharding import PartitionSpec as P

HQ = 32
HK = 4
HD = 128
TOK = 128
RATIO = HQ // HK
PAIRS = RATIO // 2
HALF = HD // 2
ROPE_BASE = 1000000.0
TRAINED_CONTEXT = 32768.0
YARN_FACTOR = 4.0
NEG_LARGE = -1.0e30
SCALE = HD**-0.5
N_LONG = 3
CHAIN = 16
SIDE = (7, 10)
RELAY = 1
MESH = pl.DeviceIdType.MESH
F32 = jnp.float32
BF16 = jnp.bfloat16


def yarn_frequencies():
    def correction(rotations):
        return HD * math.log(TRAINED_CONTEXT / (rotations * 2.0 * math.pi)) / (2.0 * math.log(ROPE_BASE))

    lower = max(math.floor(correction(32.0)), 0)
    upper = min(math.ceil(correction(1.0)), HD - 1)
    spread = max(upper - lower, 0.001)
    index = np.arange(HALF, dtype=np.float64)
    base = ROPE_BASE ** (-2.0 * index / HD)
    ramp = np.clip((index - lower) / spread, 0.0, 1.0)
    return (base / YARN_FACTOR * ramp + base * (1.0 - ramp)).astype(np.float32)


def sin_cos(x):
    n = jnp.floor(x * (2.0 / math.pi) + 0.5)
    r = x - n * 1.5703125
    r = r - n * 4.83751296997070312e-4
    r = r - n * 7.54978995489188216e-8
    z = r * r
    sin = r + r * z * (-1.6666654611e-1 + z * (8.3321608736e-3 + z * -1.9515295891e-4))
    cos = 1.0 - 0.5 * z + z * z * (4.166664568298827e-2 + z * (-1.388731625493765e-3 + z * 2.443315711809948e-5))
    q = n.astype(jnp.int32) & 3
    odd = (q & 1) == 1
    s = jnp.where(odd, cos, sin)
    c = jnp.where(odd, sin, cos)
    return jnp.where(q >= 2, -s, s), jnp.where((q == 1) | (q == 2), -c, c)


def long_pair(i, early):
    return i * PAIRS + 1 - jnp.minimum(i, 1) - 2 * early * (i // 2)


def dot_t(a, b):
    return lax.dot_general(a, b, (((1,), (1,)), ((), ())), preferred_element_type=F32)


def dot(a, b):
    return jnp.dot(a, b, preferred_element_type=F32)


def kernel(
    n_ctx,
    doc_hbm, fetch_hbm, freq_hbm, q_hbm, k_hbm, v_hbm, o_hbm, do_hbm,
    out_ref, dk_ref, dv_ref,
    doc_ref, fetch_ref, freq_ref, q_in, o_in, do_in,
    kv, qr, doz, bias, tab_t, tab_c, tab_s, k_t, p_win, ds_win, own, back_out, back_in, dq, relay, side,
    ready, helped, small_sem, kv_sem, query_sem, kv_send, kv_recv, back_send, back_recv, dq_send, out_recv, relay_recv, relay_send, side_recv, side_send,
):
    c = lax.axis_index("ctx")
    s = lax.axis_index("section")

    place = lax.rem(c, CHAIN)
    first_chip = (place < 2) & (s >= 1)
    helps = [(place // 2 == i + 1) & (s <= 2) for i in range(len(SIDE))]

    small = [
        pltpu.make_async_copy(doc_hbm, doc_ref, small_sem.at[0]),
        pltpu.make_async_copy(freq_hbm, freq_ref, small_sem.at[1]),
        pltpu.make_async_copy(fetch_hbm, fetch_ref, small_sem.at[2]),
    ]

    def head_cols(ref, g):
        return ref.at[0, :, pl.ds(pl.multiple_of(g * HD, HD), HD)]

    def kv_loads(g):
        return [
            pltpu.make_async_copy(head_cols(x, g), kv.at[0, g, i], kv_sem.at[i, g]) for i, x in enumerate((k_hbm, v_hbm))
        ]

    def query_loads(g):
        cols = pl.ds(pl.multiple_of(g * RATIO * HD, RATIO * HD), RATIO * HD)
        return [
            pltpu.make_async_copy(x.at[0, :, cols], y.at[g], query_sem.at[i, g])
            for i, (x, y) in enumerate(((q_hbm, q_in), (do_hbm, do_in), (o_hbm, o_in)))
        ]

    for load in small:
        load.start()
    for g in range(HK):
        for load in kv_loads(g) + query_loads(g):
            load.start()

    barrier = pltpu.get_barrier_semaphore()
    for d in (1, 2):
        @pl.when(c >= d)
        def _():
            pl.semaphore_signal(barrier, inc=1, device_id=(c - d, s), device_id_type=MESH)
    for me, others in ((0, (1, 2, 3)), (1, (2,)), (2, (3,))):
        @pl.when(s == me)
        def _():
            for other in others:
                pl.semaphore_signal(barrier, inc=1, device_id=(c, other), device_id_type=MESH)

    @pl.when(first_chip)
    def _():
        for i in range(len(SIDE)):
            pl.semaphore_signal(barrier, inc=1, device_id=(c + 2 * i + 2, s - 1), device_id_type=MESH)

    greeted = s - s // 3 + sum(h.astype(jnp.int32) for h in helps) + (c < n_ctx - 1).astype(jnp.int32) + (c < n_ctx - 2).astype(jnp.int32)

    @pl.when(greeted > 0)
    def _():
        pl.semaphore_wait(barrier, greeted)

    for me, others in ((1, (0,)), (2, (0, 1))):
        @pl.when(s == me)
        def _():
            for other in others:
                pl.semaphore_signal(ready, inc=1, device_id=(c, other), device_id_type=MESH)

    for i in range(len(SIDE)):
        @pl.when(helps[i])
        def _():
            pl.semaphore_signal(helped, inc=1, device_id=(c - 2 * i - 2, s + 1), device_id_type=MESH)

    def kv_copies(g, d):
        return [
            pltpu.make_async_remote_copy(
                src_ref=head_cols(x, g), dst_ref=kv.at[d, g, i],
                send_sem=kv_send.at[d - 1, g, i], recv_sem=kv_recv.at[d - 1, g, i],
                device_id=(c + d, s), device_id_type=MESH,
            )
            for i, x in enumerate((k_hbm, v_hbm))
        ]

    for i in range(2):
        for d in (1, 2):
            pl.when(c < n_ctx - d)(kv_copies(0, d)[i].start)
    for d in (1, 2):
        @pl.when(c < d)
        def _():
            kv[d] = jnp.zeros((HK, 2, TOK, HD), BF16)
        @pl.when(c >= n_ctx - d)
        def _():
            back_in[d - 1] = jnp.zeros((HK, 2, TOK, HD), BF16)

    for load in small:
        load.wait()
    first = c * TOK
    lane = lax.broadcasted_iota(jnp.int32, (1, TOK), 1)
    lane_t = lane + first
    start = doc_ref[...]
    factor = 0.1 * math.log(YARN_FACTOR) + 1.0
    low = lax.broadcasted_iota(jnp.int32, (TOK, HD), 1) < HALF
    for d in range(3):
        position = lane_t - start if d == 0 else jnp.maximum(lane_t - d * TOK - start[:, 0:1], 0)
        sin, cos = sin_cos(position.astype(F32) * freq_ref[...])
        sin = sin * factor
        cos = cos * factor
        if d == 0:
            tab_t[0] = cos * SCALE
            tab_t[1] = sin * SCALE
        turned = jnp.concatenate([cos, sin], axis=0).T
        swapped = pltpu.roll(turned, HALF, 1)
        tab_c[d] = jnp.where(low, turned, swapped)
        tab_s[d] = jnp.where(low, -swapped, turned)

    def rope(x, d):
        x = x.astype(F32)
        return (x * tab_c[d] + pltpu.roll(x, HALF, 1) * tab_s[d]).astype(BF16)

    def zero_copy(p):
        return pltpu.make_async_copy(
            relay.at[0, 0], out_ref.at[0, :, pl.ds(pl.multiple_of(p * 2 * HD, 2 * HD), 2 * HD)], out_recv.at[p]
        )

    @pl.when(s == 3)
    def _():
        relay[0, 0] = jnp.zeros((TOK, 2 * HD), BF16)

        def put(p, carry):
            zero_copy(p).start()
            return carry

        lax.fori_loop(0, HK * PAIRS, put, 0)

    row = lax.broadcasted_iota(jnp.int32, (TOK, TOK), 0)
    for d in range(3):
        u = first - d * TOK + row
        allowed = (u >= start) & (u <= lane_t)
        if d > 0:
            allowed = allowed & (fetch_ref[:, d - 1 : d] == 1)
        bias[d * TOK : (d + 1) * TOK, :] = jnp.where(allowed, 0.0, NEG_LARGE)

    for g in range(HK):
        for load in query_loads(g) + kv_loads(g):
            load.wait()

    def prepare(g):
        for i in range(RATIO):
            h = g * RATIO + i
            cols = slice(i * HD, (i + 1) * HD)
            qr[h] = rope(q_in[g, :, cols], 0)
            grad = do_in[g, :, cols]
            prod = grad.astype(F32) * o_in[g, :, cols].astype(F32)
            prod = prod + pltpu.roll(prod, HALF, 1)
            high = prod.astype(BF16).astype(F32)
            doz[h, :, 0:HD] = grad
            doz[h, :, HD : 2 * HD] = jnp.where(low, high, prod - high).astype(BF16)

    lax.fori_loop(0, HK, lambda g, c: (prepare(g), c)[1], 0)

    for g in range(1, HK):
        for d in (1, 2):
            @pl.when(c < n_ctx - d)
            def _():
                for copy in kv_copies(g, d):
                    copy.start()

    def out_cols(p):
        return out_ref.at[0, :, pl.ds(pl.multiple_of(p * 2 * HD, 2 * HD), 2 * HD)]

    def direct_copy(p):
        return pltpu.make_async_remote_copy(
            src_ref=dq.at[p], dst_ref=out_cols(p), send_sem=dq_send.at[p], recv_sem=out_recv.at[p],
            device_id=(c, s - 1), device_id_type=MESH,
        )

    def long_copy(g):
        return pltpu.make_async_remote_copy(
            src_ref=dq.at[long_pair(g, s // 3)], dst_ref=relay.at[s // 3, g],
            send_sem=dq_send.at[long_pair(g, s // 3)], recv_sem=relay_recv.at[s // 3, g],
            device_id=(c, 2 * (1 - s // 2)), device_id_type=MESH,
        )

    def side_copy(i):
        return pltpu.make_async_remote_copy(
            src_ref=dq.at[SIDE[i]], dst_ref=side.at[i],
            send_sem=dq_send.at[SIDE[i]], recv_sem=side_recv.at[i],
            device_id=(c + 2 * i + 2, s - 1), device_id_type=MESH,
        )

    def side_back(i):
        return pltpu.make_async_remote_copy(
            src_ref=side.at[i], dst_ref=out_cols(SIDE[i]),
            send_sem=side_send.at[i], recv_sem=out_recv.at[SIDE[i]],
            device_id=(c - 2 * i - 2, s), device_id_type=MESH,
        )

    def relay_copy(slot, g, target):
        p = long_pair(g, slot)
        return pltpu.make_async_remote_copy(
            src_ref=relay.at[slot, g], dst_ref=out_cols(p),
            send_sem=relay_send.at[slot, g], recv_sem=out_recv.at[p],
            device_id=(c, target), device_id_type=MESH,
        )

    def arrival(slot, g):
        return pltpu.make_async_remote_copy(
            src_ref=dq.at[0], dst_ref=relay.at[slot, g],
            send_sem=dq_send.at[0], recv_sem=relay_recv.at[slot, g],
            device_id=(c, 0), device_id_type=MESH,
        )

    def forward(g):
        @pl.when(s == 0)
        def _():
            @pl.when(g == 0)
            def _():
                pl.semaphore_wait(ready, 2)

            arrival(0, g).wait_recv()
            relay_copy(0, g, 1).start()
            arrival(1, g).wait_recv()
            relay_copy(1, g, 2).start()

        @pl.when(s == 2)
        def _():
            arrival(0, g).wait_recv()
            relay_copy(0, g, 0).start()

    def back_copy(g, d):
        return pltpu.make_async_remote_copy(
            src_ref=back_out.at[d - 1, g], dst_ref=back_in.at[d - 1, g],
            send_sem=back_send.at[d - 1, g], recv_sem=back_recv.at[d - 1, g],
            device_id=(c - d, s), device_id_type=MESH,
        )

    def group(g, carry):
        for d in (1, 2):
            pl.when(c >= d)(kv_copies(g, d)[0].wait_recv)
        k_win = jnp.concatenate([rope(kv[d, g, 0], d) for d in range(3)], axis=0)
        k_t[...] = k_win.T
        first_scores = dot_t(k_win, qr[pl.ds(g * RATIO, 2)].reshape(2 * TOK, HD))
        for d in (1, 2):
            pl.when(c >= d)(kv_copies(g, d)[1].wait_recv)
        v_win = jnp.concatenate([kv[d, g, 1] for d in range(3)], axis=0)
        v_one = jnp.concatenate([v_win, jnp.full((3 * TOK, HD), -1.0, BF16)], axis=1)
        b = bias[...]
        b = jnp.concatenate([b, b], axis=1)

        def products(j):
            h = g * RATIO + 2 * j
            qp = qr[pl.ds(h, 2)].reshape(2 * TOK, HD)
            dp_in = doz[pl.ds(h, 2)].reshape(2 * TOK, 2 * HD)
            return first_scores if j == 0 else dot_t(k_win, qp), dot_t(v_one, dp_in)

        ahead = products(0)
        for j in range(PAIRS):
            p = g * PAIRS + j
            sc, dp = ahead
            if j + 1 < PAIRS:
                ahead = products(j + 1)
            sc = sc * (SCALE * math.log2(math.e)) + b
            e = jnp.exp2(sc - jnp.max(sc, axis=0, keepdims=True))
            prob = e * (1.0 / jnp.sum(e, axis=0, keepdims=True))
            ds = (prob * dp).astype(BF16)
            p_win[:, 2 * j * TOK : 2 * (j + 1) * TOK] = prob.astype(BF16)
            ds_win[:, 2 * j * TOK : 2 * (j + 1) * TOK] = ds
            if j == 0:
                @pl.when(first_chip & (g == 1))
                def _():
                    pl.semaphore_wait(helped, len(SIDE))

            if j == 1:
                @pl.when((s == 1) & (g == 0))
                def _():
                    pl.semaphore_wait(ready, 1)

            @pl.when(s >= 1)
            def _():
                turned_grad = dot(k_t[...], ds_win[:, 2 * j * TOK : 2 * (j + 1) * TOK])
                for i in range(2):
                    x = turned_grad[:HALF, i * TOK : (i + 1) * TOK]
                    y = turned_grad[HALF:, i * TOK : (i + 1) * TOK]
                    grad = jnp.concatenate(
                        [x * tab_t[0] + y * tab_t[1], y * tab_t[0] - x * tab_t[1]], axis=0
                    )
                    dq[p, :, i * HD : (i + 1) * HD] = grad.T.astype(BF16)
                if j == 0:
                    far = (g == 1) | ((g == 2) & (s < 3))
                    pl.when(far)(long_copy(g).start)
                    pl.when(jnp.logical_not(far))(direct_copy(p).start)
                elif j == 1:
                    pl.when(g == 0)(long_copy(g).start)
                    pl.when(g >= 1)(direct_copy(p).start)
                elif j == 2:
                    far = (g == 1) & (s == 3)
                    aside = (g == 2) & first_chip
                    pl.when(far)(long_copy(2).start)
                    pl.when(aside)(side_copy(1).start)
                    pl.when(((g < 3) | first_chip) & jnp.logical_not(far | aside))(direct_copy(p).start)
                else:
                    aside = (g == 1) & first_chip
                    pl.when(aside)(side_copy(0).start)
                    pl.when(((g < 2) | first_chip) & jnp.logical_not(aside))(direct_copy(p).start)

        dk = dot(ds_win[...], qr[pl.ds(g * RATIO, RATIO)].reshape(RATIO * TOK, HD))
        dv = dot(p_win[...], doz[pl.ds(g * RATIO, RATIO), :, 0:HD].reshape(RATIO * TOK, HD))
        own[g, 0] = dk[:TOK]
        own[g, 1] = dv[:TOK]
        for d in (1, 2):
            back_out[d - 1, g, 0] = dk[d * TOK : (d + 1) * TOK].astype(BF16)
            back_out[d - 1, g, 1] = dv[d * TOK : (d + 1) * TOK].astype(BF16)
            pl.when(c >= d)(back_copy(g, d).start)

        pl.when((s == 2) & (g >= 1))(lambda: forward(g - 1))
        due = g - 2

        @pl.when((s == 0) & (due >= 0))
        def _():
            forward(due)

        return carry

    lax.fori_loop(0, HK, group, 0)

    pl.when(s == 0)(lambda: forward(N_LONG - 1))


    for i, rest in enumerate(((11,), (14, 15))):
        @pl.when(helps[i])
        def _():
            side_copy(i).wait_recv()
            side_back(i).start()

        @pl.when((s >= 1) & jnp.logical_not(first_chip))
        def _():
            for p in rest:
                direct_copy(p).start()


    def finish(g, carry):
        for d in (1, 2):
            pl.when(c < n_ctx - d)(back_copy(g, d).wait_recv)
        dk = own[g, 0] + back_in[0, g, 0].astype(F32) + back_in[1, g, 0].astype(F32)
        dv = own[g, 1] + back_in[0, g, 1].astype(F32) + back_in[1, g, 1].astype(F32)
        dk = dk * SCALE
        cols = pl.ds(pl.multiple_of(g * HD, HD), HD)
        dk_ref[0, :, cols] = (dk * tab_c[0] - pltpu.roll(dk, HALF, 1) * tab_s[0]).astype(BF16)
        dv_ref[0, :, cols] = dv.astype(BF16)
        return carry

    lax.fori_loop(0, HK, finish, 0)

    def drain(g, carry):
        for d in (1, 2):
            @pl.when(c < n_ctx - d)
            def _():
                for copy in kv_copies(g, d):
                    copy.wait_send()

            pl.when(c >= d)(back_copy(g, d).wait_send)

        @pl.when(s >= 1)
        def _():
            for j in range(PAIRS):
                direct_copy(g * PAIRS + j).wait_send()

        @pl.when((s == 0) & (g < N_LONG))
        def _():
            relay_copy(0, g, 1).wait_send()
            relay_copy(1, g, 2).wait_send()

        @pl.when((s == 2) & (g < N_LONG))
        def _():
            relay_copy(0, g, 0).wait_send()

        @pl.when(s <= 2)
        def _():
            for j in range(PAIRS):
                direct_copy(g * PAIRS + j).wait_recv()

        @pl.when(s == 3)
        def _():
            for j in range(PAIRS):
                zero_copy(g * PAIRS + j).wait()

        return carry

    lax.fori_loop(0, HK, drain, 0)

    for i in range(len(SIDE)):
        pl.when(helps[i])(side_back(i).wait_send)


def hand_out(a, b, c, a_out, b_out, c_out, sem):
    copies = [
        pltpu.make_async_copy(b, b_out, sem.at[0]),
        pltpu.make_async_copy(c, c_out, sem.at[1]),
    ]
    copies.append(pltpu.make_async_copy(a, a_out, sem.at[2]))
    for copy in copies:
        copy.start()
    for copy in copies:
        copy.wait()


def solution(mesh):
    n_ctx = mesh.shape["ctx"]
    freq = np.broadcast_to(yarn_frequencies()[:, None], (HALF, TOK)).copy()

    def shards(q, k, v, o, do, doc_start, fetch_list):
        any_spec = pl.BlockSpec(memory_space=pl.ANY)
        hbm = pl.BlockSpec(memory_space=pltpu.HBM)
        vmem = pl.BlockSpec(memory_space=pltpu.VMEM)
        dma = pltpu.SemaphoreType.DMA
        results = pl.pallas_call(
            functools.partial(kernel, n_ctx),
            out_shape=(
                pltpu.VMEM((1, TOK, HQ * HD), BF16),
                pltpu.VMEM((1, TOK, HK * HD), BF16),
                pltpu.VMEM((1, TOK, HK * HD), BF16),
            ),
            in_specs=[hbm] * 8,
            out_specs=(vmem,) * 3,
            scratch_shapes=[
                pltpu.VMEM((1, TOK), jnp.int32),
                pltpu.VMEM((1, 2), jnp.int32),
                pltpu.VMEM((HALF, TOK), F32),
                pltpu.VMEM((HK, TOK, RATIO * HD), BF16),
                pltpu.VMEM((HK, TOK, RATIO * HD), BF16),
                pltpu.VMEM((HK, TOK, RATIO * HD), BF16),
                pltpu.VMEM((3, HK, 2, TOK, HD), BF16),
                pltpu.VMEM((HQ, TOK, HD), BF16),
                pltpu.VMEM((HQ, TOK, 2 * HD), BF16),
                pltpu.VMEM((3 * TOK, TOK), F32),
                pltpu.VMEM((2, HALF, TOK), F32),
                pltpu.VMEM((3, TOK, HD), F32),
                pltpu.VMEM((3, TOK, HD), F32),
                pltpu.VMEM((HD, 3 * TOK), BF16),
                pltpu.VMEM((3 * TOK, RATIO * TOK), BF16),
                pltpu.VMEM((3 * TOK, RATIO * TOK), BF16),
                pltpu.VMEM((HK, 2, TOK, HD), F32),
                pltpu.VMEM((2, HK, 2, TOK, HD), BF16),
                pltpu.VMEM((2, HK, 2, TOK, HD), BF16),
                pltpu.VMEM((HK * PAIRS, TOK, 2 * HD), BF16),
                pltpu.VMEM((2, HK, TOK, 2 * HD), BF16),
                pltpu.VMEM((len(SIDE), TOK, 2 * HD), BF16),
                pltpu.SemaphoreType.REGULAR,
                pltpu.SemaphoreType.REGULAR,
                dma((3,)),
                dma((2, HK)),
                dma((3, HK)),
                dma((2, HK, 2)),
                dma((2, HK, 2)),
                dma((2, HK)),
                dma((2, HK)),
                dma((HK * PAIRS,)),
                dma((HK * PAIRS,)),
                dma((2, HK)),
                dma((2, HK)),
                dma((len(SIDE),)),
                dma((len(SIDE),)),
            ],
            compiler_params=pltpu.CompilerParams(
                collective_id=0, has_side_effects=True, vmem_limit_bytes=28 << 20
            ),
            cost_estimate=pl.CostEstimate(flops=2_000_000_000, bytes_accessed=5_000_000, transcendentals=1_600_000),
        )(*(pltpu.with_memory_space_constraint(x, pltpu.HBM) for x in (doc_start.reshape(1, TOK), fetch_list, jnp.asarray(freq), q, k, v, o, do)))
        return pl.pallas_call(
            hand_out,
            out_shape=tuple(jax.ShapeDtypeStruct((1, TOK, n * HD), BF16) for n in (HQ, HK, HK)),
            in_specs=[vmem] * 3,
            out_specs=(hbm,) * 3,
            scratch_shapes=[dma((3,))],
            compiler_params=pltpu.CompilerParams(vmem_limit_bytes=1 << 20),
            cost_estimate=pl.CostEstimate(flops=0, bytes_accessed=2_600_000, transcendentals=0),
        )(*results)

    return jax.shard_map(
        shards,
        mesh=mesh,
        in_specs=(
            P("section", "ctx", None),
            P("section", "ctx", None),
            P("section", "ctx", None),
            P("section", "ctx", None),
            P("section", "ctx", None),
            P("ctx"),
            P("ctx", None),
        ),
        out_specs=(P("section", "ctx", None),) * 3,
        check_vma=False,
    )
```
